32 devices in a mesh: dp: 8 (over z, x), tensor: 4 (over y, core).
Axes of the slice: x: 2, y: 2, z: 4, core: 2. Of those that a mesh axis runs over, the one named last changes fastest.
Arguments:
- inputs: bfloat16 [16, 256, 2048], P('dp', 'tensor'), may hold values from -36 to 36
- attn_norm: bfloat16 [2048], P('dp'), may hold values from 0.5 to 1.5
- query_weight: bfloat16 [2048, 1280], P('dp', 'tensor'), may hold values from -0.125 to 0.125
- key_value_weight: bfloat16 [2048, 640], P('dp'), may hold values from -0.125 to 0.125
- out_weight: bfloat16 [1280, 2048], P('tensor', 'dp'), may hold values from -0.625 to 0.625
- ffn_norm: bfloat16 [2048], P('dp'), may hold values from 0.5 to 1.5
- gate_weight: bfloat16 [2048, 2816], P('dp', 'tensor'), may hold values from -0.125 to 0.125
- up_weight: bfloat16 [2048, 2816], P('dp', 'tensor'), may hold values from -0.125 to 0.125
- down_weight: bfloat16 [2816, 2048], P('tensor', 'dp'), may hold values from -0.109375 to 0.109375
- query_gain: bfloat16 [64], replicated, may hold values from 0.099609375 to 1.8984375
- key_gain: bfloat16 [64], replicated, may hold values from 0.099609375 to 1.8984375
- cotangent: bfloat16 [16, 256, 2048], P('dp', 'tensor'), may hold values from -6 to 6
Outputs:
- output: bfloat16 [16, 256, 2048], P('dp', 'tensor')
- input_grad: float32 [16, 256, 2048], P('dp', 'tensor')
- attn_norm_grad: float32 [2048], P('dp')
- query_weight_grad: float32 [2048, 1280], P('dp', 'tensor')
- kv_weight_grad: float32 [2048, 640], P('dp')
- out_weight_grad: float32 [1280, 2048], P('tensor', 'dp')
- ffn_norm_grad: float32 [2048], P('dp')
- gate_weight_grad: float32 [2048, 2816], P('dp', 'tensor')
- up_weight_grad: float32 [2048, 2816], P('dp', 'tensor')
- down_weight_grad: float32 [2816, 2048], P('tensor', 'dp')
- query_gain_grad: float32 [64], replicated
- key_gain_grad: float32 [64], replicated
The draws below stay inside these ranges and needn't reach their ends.
All inputs are finite; a program needn't handle non-finite values.
Results may differ from the reference program's by a relative error of at most 0.02.
Values may be sent and summed in bfloat16 or wider, within the bound.
No kernel may reach another device: no remote copies, remote signals or barrier semaphores. Data moves between devices by JAX's collectives and lax.ppermute only.
A program may use at most 128 MiB of HBM per device.

```python
import math
import jax
import jax.numpy as jnp
from jax import lax

MODEL_WIDTH = 2048
QUERY_HEADS = 20
KEY_VALUE_HEADS = 5
HEAD_WIDTH = 64
FF = 2816
SEQ = 256
SEQS = 16


def draw_inputs(key, part):
    key = jax.random.fold_in(key, 7)
    base_key, row_key, column_key = jax.random.split(key, 3)
    full_shape = (SEQS, SEQ, MODEL_WIDTH)
    entries = jnp.clip(jax.random.normal(base_key, full_shape, jnp.float32), -4.0, 4.0)
    lower_end = math.log(0.3)
    upper_end = math.log(3.0)
    row_scale = jnp.exp(jax.random.uniform(row_key, (SEQS, SEQ, 1), jnp.float32, lower_end, upper_end))
    column_scale = jnp.exp(jax.random.uniform(column_key, (1, 1, MODEL_WIDTH), jnp.float32, lower_end, upper_end))
    return (entries * row_scale * column_scale).astype(jnp.bfloat16)


def spiked(values, stream_key, source, target, shards_of, factor):
    owner, partner = [(jnp.arange(values.shape[position]) // (values.shape[position] // shards_of)).reshape([-1 if axis == position else 1 for axis in range(values.ndim)]) for position in (source, target)]
    chosen = jax.random.permutation(stream_key, shards_of)[partner]
    strong = (owner == chosen) | (owner == (partner + shards_of // 2) % shards_of)
    return jnp.where(strong, factor * values, values)


def steps_of(rng, dims, shards, low, high):
    def one(position, blocks):
        steps = jax.random.uniform(jax.random.fold_in(jax.random.fold_in(rng, 6), position), (blocks,), jnp.float32, low / len(shards), high / len(shards))
        return jnp.repeat(jnp.exp(steps), dims[position] // blocks).reshape((-1,) + (1,) * (len(dims) - position - 1))

    factor_of = one(*shards[0])
    for cut in shards[1:]:
        factor_of = factor_of * one(*cut)
    return factor_of


def scatter_about(rng, shape, spread, bound, cuts=(), held_as=jnp.bfloat16):
    array = jax.random.normal(rng, shape, jnp.float32) * spread
    if len(cuts) > 0:
        array = steps_of(rng, shape, cuts, -0.22, 0.18) * array
    return jnp.clip(array, min=-bound, max=bound).astype(held_as)


def noise_with(stream_key, extent, spread, most, cuts, heavy, kind=jnp.bfloat16):
    drawn = spread * jax.random.normal(stream_key, extent, jnp.float32)
    if cuts:
        drawn = drawn * steps_of(stream_key, extent, cuts, -0.22, 0.18)
    return jnp.clip(spiked(drawn, jax.random.fold_in(stream_key, 3), *heavy), -most, most).astype(kind)


def setup_inputs(seed: int = 0) -> dict:
    streams_of = jax.random.split(jax.random.key(seed), 13)
    return {
        "inputs": draw_inputs(jax.random.fold_in(streams_of[12], 71), 0),
        "attn_norm": jnp.clip(1.0 + 0.1 * jax.random.normal(streams_of[1], (MODEL_WIDTH,), jnp.float32), 0.5, 1.5).astype(jnp.bfloat16),
        "query_weight": scatter_about(streams_of[2], (MODEL_WIDTH, QUERY_HEADS * HEAD_WIDTH), MODEL_WIDTH ** -0.5, 0.125, ((0, 8), (1, 4))),
        "key_value_weight": scatter_about(streams_of[3], (MODEL_WIDTH, 2 * KEY_VALUE_HEADS * HEAD_WIDTH), MODEL_WIDTH ** -0.5, 0.125, ((0, 8),)),
        "out_weight": scatter_about(streams_of[4], (QUERY_HEADS * HEAD_WIDTH, MODEL_WIDTH), (QUERY_HEADS * HEAD_WIDTH // 16) ** -0.5, 0.625, ((0, 4), (1, 8))),
        "ffn_norm": jnp.clip(1.0 + 0.1 * jax.random.normal(streams_of[5], (MODEL_WIDTH,), jnp.float32), 0.5, 1.5).astype(jnp.bfloat16),
        "gate_weight": scatter_about(streams_of[6], (MODEL_WIDTH, FF), MODEL_WIDTH ** -0.5, 0.125, ((0, 8), (1, 4))),
        "up_weight": scatter_about(streams_of[7], (MODEL_WIDTH, FF), MODEL_WIDTH ** -0.5, 0.125, ((0, 8), (1, 4))),
        "down_weight": scatter_about(streams_of[8], (FF, MODEL_WIDTH), FF ** -0.5, 0.109375, ((0, 4), (1, 8))),
        "query_gain": jnp.clip(1.0 + 0.18 * jax.random.normal(streams_of[9], (HEAD_WIDTH,), jnp.float32), 0.099609375, 1.8984375).astype(jnp.bfloat16),
        "key_gain": jnp.clip(1.0 + 0.18 * jax.random.normal(streams_of[10], (HEAD_WIDTH,), jnp.float32), 0.099609375, 1.8984375).astype(jnp.bfloat16),
        "cotangent": noise_with(streams_of[11], (SEQS, SEQ, MODEL_WIDTH), 1.0, 6.0, ((0, 8), (1, 4)), (0, 2, 8, 2.0)),
    }


norm_eps = 1e-06
rope_base = 10000.0
masked_score = -1e+30

@jax.custom_vjp
def reduced_copy(v):
    return lax.optimization_barrier(v.astype(jnp.bfloat16)).astype(jnp.float32)

@jax.custom_vjp
def low_back(v):
    return v

def low_keep(v):
    return (reduced_copy(v), None)

def low_pass(kept, grad):
    return (grad,)

def back_keep(v):
    return (v, None)

def back_low(kept, grad):
    return (reduced_copy(grad),)
reduced_copy.defvjp(low_keep, low_pass)
low_back.defvjp(back_keep, back_low)

def matmul_high(left, right):
    return jnp.dot(left, right, precision=lax.Precision.HIGHEST)

def rms_scale(value_tensors, gain):
    mean_square = lax.optimization_barrier(jnp.mean(value_tensors * value_tensors, axis=-1, keepdims=True))
    return value_tensors * lax.rsqrt(mean_square + norm_eps) * gain

def rope_tables(token_length, head_size):
    half_size = head_size // 2
    inverse = rope_base ** (-2.0 * jnp.arange(half_size, dtype=jnp.float32) / head_size)
    angles = jnp.arange(token_length, dtype=jnp.float32)[:, None] * inverse[None, :]
    cosine = jnp.concatenate([jnp.cos(angles), jnp.cos(angles)], axis=-1)
    sine = jnp.concatenate([jnp.sin(angles), jnp.sin(angles)], axis=-1)
    return (cosine, sine)

def rotate(value_tensors, cosine, sine):
    half_size = value_tensors.shape[-1] // 2
    turned = jnp.concatenate([-value_tensors[..., half_size:], value_tensors[..., :half_size]], axis=-1)
    return value_tensors * cosine[:, None, :] + turned * sine[:, None, :]

def layer(tokens, params):
    attn_norm, query_weight, key_value_weight, out_weight, ffn_norm, gate_weight, up_weight, down_weight, query_gain, key_gain = params
    token_length = tokens.shape[0]
    normed = reduced_copy(rms_scale(tokens, attn_norm))
    queries = low_back(matmul_high(normed, query_weight)).reshape(token_length, QUERY_HEADS, HEAD_WIDTH)
    key_value_pairs = low_back(matmul_high(normed, key_value_weight))
    key_tensors = key_value_pairs[:, :KEY_VALUE_HEADS * HEAD_WIDTH].reshape(token_length, KEY_VALUE_HEADS, HEAD_WIDTH)
    value_tensors = reduced_copy(key_value_pairs[:, KEY_VALUE_HEADS * HEAD_WIDTH:]).reshape(token_length, KEY_VALUE_HEADS, HEAD_WIDTH)
    cosine, sine = rope_tables(token_length, HEAD_WIDTH)
    queries = reduced_copy(rotate(rms_scale(queries, query_gain), cosine, sine))
    key_tensors = reduced_copy(rotate(rms_scale(key_tensors, key_gain), cosine, sine))
    key_tensors = jnp.repeat(key_tensors, QUERY_HEADS // KEY_VALUE_HEADS, axis=1)
    value_tensors = jnp.repeat(value_tensors, QUERY_HEADS // KEY_VALUE_HEADS, axis=1)
    scores = low_back(jnp.einsum('qhd,khd->hqk', queries, key_tensors, precision=lax.Precision.HIGHEST) * HEAD_WIDTH ** (-0.5))
    causal = jnp.arange(token_length)[:, None] >= jnp.arange(token_length)[None, :]
    scores = jnp.where(causal[None], scores, masked_score)
    probs = reduced_copy(jax.nn.softmax(scores, axis=-1))
    mixed = jnp.einsum('hqk,khd->qhd', probs, value_tensors, precision=lax.Precision.HIGHEST)
    mixed = reduced_copy(low_back(mixed)).reshape(token_length, QUERY_HEADS * HEAD_WIDTH)
    middle = tokens + low_back(matmul_high(mixed, out_weight))
    normed_ffn = reduced_copy(rms_scale(middle, ffn_norm))
    gate = low_back(matmul_high(normed_ffn, gate_weight))
    upward = low_back(matmul_high(normed_ffn, up_weight))
    hidden = reduced_copy(jax.nn.silu(gate) * upward)
    return middle + low_back(matmul_high(hidden, down_weight))

def reference(inputs, attn_norm, query_weight, key_value_weight, out_weight, ffn_norm, gate_weight, up_weight, down_weight, query_gain, key_gain, cotangent):
    weights = tuple((weight.astype(jnp.float32) for weight in (attn_norm, query_weight, key_value_weight, out_weight, ffn_norm, gate_weight, up_weight, down_weight, query_gain, key_gain)))
    pack_size = math.gcd(SEQS, max(1, 4096 // SEQ))
    grouped = inputs.astype(jnp.float32).reshape(SEQS // pack_size, pack_size, SEQ, MODEL_WIDTH)

    def forward(all_tokens, params):
        step_function = jax.checkpoint(jax.vmap(layer, in_axes=(0, None)))

        def advance(running_total, group):
            return (running_total, step_function(group, params))
        _, results = lax.scan(advance, jnp.zeros((), jnp.float32), all_tokens)
        return results
    results, pullback = jax.vjp(forward, grouped, weights)
    grad_inputs, grad_weights = pullback(cotangent.astype(jnp.float32).reshape(grouped.shape))
    return (results.reshape(SEQS, SEQ, MODEL_WIDTH).astype(jnp.bfloat16), grad_inputs.reshape(SEQS, SEQ, MODEL_WIDTH), grad_weights[0], grad_weights[1], grad_weights[2], grad_weights[3], grad_weights[4], grad_weights[5], grad_weights[6], grad_weights[7], grad_weights[8], grad_weights[9])
```

```python
from functools import partial

import jax
import jax.numpy as jnp
import numpy as np
from jax import lax
from jax.sharding import PartitionSpec as P

norm_eps = 1e-06
rope_base = 10000.0
masked_score = -1e30
f32 = jnp.float32
bf16 = jnp.bfloat16

RING = (0, 2, 4, 6, 7, 5, 3, 1)
OFFSETS = (0, -1, 1, -2, 2, -3, 3, 4)
PLACE = {ring: slot for slot, ring in enumerate(OFFSETS)}


def nn(left, right):
    return lax.dot_general(left, right, (((1,), (0,)), ((), ())), preferred_element_type=f32)


def nt(left, right):
    return lax.dot_general(left, right, (((1,), (1,)), ((), ())), preferred_element_type=f32)


def tn(left, right):
    return lax.dot_general(left, right, (((0,), (0,)), ((), ())), preferred_element_type=f32)


def ringed():
    return lax.axis_size("dp") == len(RING)


def owner_tables():
    size = len(RING)
    owners = np.zeros((size, size), np.int32)
    inverse = np.zeros((size, size), np.int32)
    for index in range(size):
        spot = RING.index(index)
        for slot, offset in enumerate(OFFSETS):
            owner = RING[(spot + offset) % size]
            owners[index, slot] = owner
            inverse[index, owner] = slot
    return owners, inverse


def reorder(rows, table):
    size = table.shape[0]
    width = rows.shape[1] // size
    picks = jnp.asarray(table)[lax.axis_index("dp")]
    return jnp.concatenate(
        [lax.dynamic_slice_in_dim(rows, picks[i] * width, width, axis=1) for i in range(size)],
        axis=1,
    )


def to_ring(rows):
    return reorder(rows, owner_tables()[0]) if ringed() else rows


def from_ring(rows):
    return reorder(rows, owner_tables()[1]) if ringed() else rows


def step(rows, forward):
    size = len(RING)
    move = 1 if forward else -1
    return lax.ppermute(
        rows, "dp", [(RING[i], RING[(i + move) % size]) for i in range(size)]
    )


def gather_weights(shard):
    if not ringed():
        return lax.all_gather(shard, "dp", axis=1, tiled=True)
    half = shard.shape[0] // 2
    parts = {0: shard}
    ahead = behind = shard
    for hop in (1, 2, 3):
        ahead = step(ahead, True)
        behind = step(behind, False)
        parts[-hop] = ahead
        parts[hop] = behind
    parts[4] = jnp.concatenate([step(ahead[:half], True), step(behind[half:], False)], axis=0)
    return jnp.concatenate([parts[offset] for offset in OFFSETS], axis=1)


def reduce_weights(grads):
    if not ringed():
        return lax.psum_scatter(
            grads.astype(bf16), "dp", scatter_dimension=1, tiled=True
        ).astype(f32)
    size = len(RING)
    width = grads.shape[1] // size
    half = grads.shape[0] // 2

    def part(offset):
        slot = PLACE[offset]
        return grads[:, slot * width : (slot + 1) * width]

    ahead = step(part(4)[:half].astype(bf16), True)
    behind = step(part(4)[half:].astype(bf16), False)
    ahead = jnp.concatenate([part(3)[:half] + ahead, part(3)[half:]], axis=0)
    behind = jnp.concatenate([part(-3)[:half], part(-3)[half:] + behind], axis=0)
    for hop in (2, 1, 0):
        ahead = step(ahead.astype(bf16), True)
        behind = step(behind.astype(bf16), False)
        if hop:
            ahead = part(hop) + ahead
            behind = part(-hop) + behind
    return part(0) + ahead + behind


def swap(rows, bit):
    count = lax.axis_size("tensor")
    return lax.ppermute(rows, "tensor", [(i, i ^ bit) for i in range(count)])


def collect(rows):
    core = swap(rows, 1)
    across = swap(rows, 2)
    return jnp.concatenate([rows, core, across, swap(across, 1)], axis=0)


def spread(partial_sums):
    count = partial_sums.shape[0] // 4
    low = partial_sums.astype(bf16)
    block = [low[i * count : (i + 1) * count] for i in range(4)]
    other = swap(jnp.concatenate([block[1], block[3]], axis=0), 1)
    kept = partial_sums[:count] + other[:count]
    sent = partial_sums[2 * count : 3 * count] + other[count:]
    return kept + swap(sent.astype(bf16), 2)


def turn(values):
    half = values.shape[-1] // 2
    return jnp.concatenate([-values[..., half:], values[..., :half]], axis=-1)


def turn_back(values):
    half = values.shape[-1] // 2
    return jnp.concatenate([values[..., half:], -values[..., :half]], axis=-1)


def head_prep(pre, gain, cosine, sine):
    scale = lax.rsqrt(jnp.mean(pre * pre, axis=-1, keepdims=True) + norm_eps)
    scaled = pre * scale * gain
    return scaled * cosine + turn(scaled) * sine, scale


def head_back(grad, pre, scale, gain, cosine, sine):
    grad = grad * cosine + turn_back(grad * sine)
    gain_grad = jnp.sum(grad * pre * scale, axis=(0, 1, 2))
    lifted = grad * gain
    back = scale * lifted - pre * (scale**3) * jnp.mean(lifted * pre, axis=-1, keepdims=True)
    return back, gain_grad


def local(
    inputs,
    attn_norm,
    query_weight,
    key_value_weight,
    out_weight,
    ffn_norm,
    gate_weight,
    up_weight,
    down_weight,
    query_gain,
    key_gain,
    cotangent,
):
    ranks = lax.axis_size("tensor")
    rank = lax.axis_index("tensor")
    seqs, span, width = inputs.shape
    head = query_gain.shape[0]
    heads = query_weight.shape[1] // head
    kv_heads = key_value_weight.shape[1] // (2 * head)
    group = heads * ranks // kv_heads
    kv_first = [(i * heads) // group for i in range(ranks)]
    kv_last = [(i * heads + heads - 1) // group for i in range(ranks)]
    kv_local = max(b - a for a, b in zip(kv_first, kv_last)) + 1
    kv_start = jnp.asarray(
        np.asarray([min(a, kv_heads - kv_local) for a in kv_first], np.int32)
    )[rank]
    kv_of = (rank * heads + jnp.arange(heads, dtype=jnp.int32)) // group - kv_start
    rows = seqs * span
    hidden_units = gate_weight.shape[1]
    q_cols = heads * head
    kv_cols = kv_local * head

    attn_gain = attn_norm.astype(f32)
    ffn_gain = ffn_norm.astype(f32)
    key_weight = lax.dynamic_slice_in_dim(key_value_weight, kv_start * head, kv_cols, axis=1)
    value_weight = lax.dynamic_slice_in_dim(
        key_value_weight, (kv_heads + kv_start) * head, kv_cols, axis=1
    )
    qkv_own = jnp.concatenate([query_weight.T, key_weight.T, value_weight.T], axis=0)
    qkv_shard = (qkv_own.astype(f32) * attn_gain[None]).astype(bf16)
    gate_shard = (gate_weight.T.astype(f32) * ffn_gain[None]).astype(bf16)
    up_shard = (up_weight.T.astype(f32) * ffn_gain[None]).astype(bf16)
    qkv_full = gather_weights(qkv_shard)
    out_full = gather_weights(out_weight)
    gate_full = gather_weights(gate_shard)
    up_full = gather_weights(up_shard)
    down_full = gather_weights(down_weight)

    tokens_low = to_ring(inputs.reshape(rows, width))
    cot_low = to_ring(cotangent.reshape(rows, width))
    tokens = tokens_low.astype(f32)
    whole = collect(tokens_low)
    cot_whole = collect(cot_low)

    block_of = rank ^ jnp.arange(ranks, dtype=jnp.int32)
    positions = (block_of[:, None] * span + jnp.arange(span, dtype=jnp.int32)[None]).reshape(-1)
    inverse = rope_base ** (-2.0 * jnp.arange(head // 2, dtype=f32) / head)
    angles = positions.astype(f32)[:, None] * inverse[None]
    cosine = jnp.concatenate([jnp.cos(angles)] * 2, axis=-1)
    sine = jnp.concatenate([jnp.sin(angles)] * 2, axis=-1)
    seq_len = ranks * span

    def by_head(flat, count):
        return (
            flat.reshape(ranks, seqs, span, count, head)
            .transpose(1, 3, 0, 2, 4)
            .reshape(seqs, count, seq_len, head)
        )

    def by_row(split):
        count = split.shape[1]
        return (
            split.reshape(seqs, count, ranks, span, head)
            .transpose(2, 0, 3, 1, 4)
            .reshape(ranks * rows, count * head)
        )

    wide = whole.astype(f32)
    row_scale = lax.rsqrt(jnp.mean(wide * wide, axis=-1, keepdims=True) + norm_eps)
    qkv = nt(whole, qkv_full) * row_scale
    query_pre = by_head(qkv[:, :q_cols], heads)
    key_pre = by_head(qkv[:, q_cols : q_cols + kv_cols], kv_local)
    values = by_head(qkv[:, q_cols + kv_cols :].astype(bf16), kv_local)
    q_gain = query_gain.astype(f32)
    k_gain = key_gain.astype(f32)
    queries, query_scale = head_prep(query_pre, q_gain, cosine, sine)
    queries = queries.astype(bf16)
    keys, key_scale = head_prep(key_pre, k_gain, cosine, sine)
    keys = keys.astype(bf16)

    picks = [kv_of[:, None] == i for i in range(kv_local)]

    def to_heads(per_kv):
        out = per_kv[:, :1]
        for i in range(1, kv_local):
            out = jnp.where(picks[i][None, :, :, None], per_kv[:, i : i + 1], out)
        return jnp.broadcast_to(out, (seqs, heads, seq_len, head))

    def to_kv(per_head):
        return jnp.stack(
            [
                jnp.sum(jnp.where(picks[i][None, :, :, None], per_head, 0.0), axis=1)
                for i in range(kv_local)
            ],
            axis=1,
        )

    keys_h = to_heads(keys)
    values_h = to_heads(values)
    scores = jnp.einsum("shqd,shkd->shqk", queries, keys_h, preferred_element_type=f32)
    scores = scores * head ** (-0.5)
    causal = positions[:, None] >= positions[None, :]
    scores = jnp.where(causal[None, None], scores, masked_score)
    expos = jnp.exp(scores - jnp.max(scores, axis=-1, keepdims=True))
    soft = expos / jnp.sum(expos, axis=-1, keepdims=True)
    probs = soft.astype(bf16)
    mixed = by_row(
        jnp.einsum("shqk,shkd->shqd", probs, values_h, preferred_element_type=f32).astype(bf16)
    )
    middle = tokens + spread(nn(mixed, out_full))
    mid_scale = lax.rsqrt(jnp.mean(middle * middle, axis=-1, keepdims=True) + norm_eps)
    ffn_whole = collect((middle * mid_scale).astype(bf16))

    gate = nt(ffn_whole, gate_full)
    upward = nt(ffn_whole, up_full)
    sig = jax.nn.sigmoid(gate)
    silu = gate * sig
    hidden = (silu * upward).astype(bf16)
    down_grad = reduce_weights(tn(hidden, cot_whole))
    result = (middle + spread(nn(hidden, down_full))).astype(bf16)

    grad_hidden = nt(cot_whole, down_full)
    grad_gate = (grad_hidden * upward * sig * (1.0 + gate * (1.0 - sig))).astype(bf16)
    grad_up = (grad_hidden * silu).astype(bf16)
    lifted = spread(nn(grad_gate, gate_full) + nn(grad_up, up_full))
    gate_grad = reduce_weights(tn(grad_gate, ffn_whole))
    up_grad = reduce_weights(tn(grad_up, ffn_whole))
    grad_middle = (
        cot_low.astype(f32)
        + mid_scale * lifted
        - middle * mid_scale**3 * jnp.mean(lifted * middle, axis=-1, keepdims=True)
    )
    grad_attn = collect(grad_middle.astype(bf16))
    out_grad = reduce_weights(tn(mixed, grad_attn))
    grad_mixed = by_head(nt(grad_attn, out_full).astype(bf16), heads)

    grad_probs = jnp.einsum("shqd,shkd->shqk", grad_mixed, values_h, preferred_element_type=f32)
    grad_scores = (
        soft * (grad_probs - jnp.sum(soft * grad_probs, axis=-1, keepdims=True))
    ).astype(bf16)
    factor = head ** (-0.5)
    grad_queries = (
        jnp.einsum("shqk,shkd->shqd", grad_scores, keys_h, preferred_element_type=f32) * factor
    )
    grad_keys = to_kv(
        jnp.einsum("shqk,shqd->shkd", grad_scores, queries, preferred_element_type=f32) * factor
    )
    grad_values = to_kv(
        jnp.einsum("shqk,shqd->shkd", probs, grad_mixed, preferred_element_type=f32)
    )
    grad_query_pre, query_gain_grad = head_back(
        grad_queries, query_pre, query_scale, q_gain, cosine, sine
    )
    grad_key_pre, key_gain_grad = head_back(
        grad_keys, key_pre, key_scale, k_gain, cosine, sine
    )
    grad_qkv = jnp.concatenate(
        [by_row(grad_query_pre), by_row(grad_key_pre), by_row(grad_values)], axis=1
    )
    grad_qkv = (grad_qkv * row_scale).astype(bf16)
    lifted_attn = spread(nn(grad_qkv, qkv_full))
    qkv_grad = reduce_weights(tn(grad_qkv, whole))
    own_scale = lax.rsqrt(jnp.mean(tokens * tokens, axis=-1, keepdims=True) + norm_eps)
    input_grad = grad_middle + lifted_attn - tokens * own_scale**2 * jnp.mean(
        lifted_attn * tokens, axis=-1, keepdims=True
    )

    attn_norm_grad = jnp.sum(qkv_grad * qkv_own.astype(f32), axis=0)
    ffn_norm_grad = jnp.sum(
        gate_grad * gate_weight.T.astype(f32) + up_grad * up_weight.T.astype(f32), axis=0
    )
    norms = jnp.stack([attn_norm_grad, ffn_norm_grad])
    norms = norms + swap(norms, 1)
    norms = norms + swap(norms, 2)
    gains = jnp.stack([query_gain_grad, key_gain_grad])
    gains = lax.psum(gains, ("dp", "tensor"))

    qkv_grad = qkv_grad * attn_gain[None]
    kv_sum = jnp.zeros((2, kv_heads * head, qkv_grad.shape[1]), f32)
    kv_own = qkv_grad[q_cols:].reshape(2, kv_cols, -1)
    kv_sum = lax.dynamic_update_slice(kv_sum, kv_own, (0, kv_start * head, 0))
    for bit in (1, 2):
        kv_sum = lax.reduce_precision(kv_sum, 8, 7)
        kv_sum = kv_sum + swap(kv_sum.astype(bf16), bit)

    return (
        from_ring(result).reshape(inputs.shape),
        from_ring(input_grad).reshape(inputs.shape),
        norms[0],
        qkv_grad[:q_cols].T,
        kv_sum.reshape(2 * kv_heads * head, -1).T,
        out_grad,
        norms[1],
        (gate_grad * ffn_gain[None]).T,
        (up_grad * ffn_gain[None]).T,
        down_grad,
        gains[0],
        gains[1],
    )


def solution(mesh):
    placed = (
        P("dp", "tensor", None),
        P("dp"),
        P("dp", "tensor"),
        P("dp", None),
        P("tensor", "dp"),
        P("dp"),
        P("dp", "tensor"),
        P("dp", "tensor"),
        P("tensor", "dp"),
        P(),
        P(),
        P("dp", "tensor", None),
    )
    return jax.shard_map(
        local,
        mesh=mesh,
        in_specs=placed,
        out_specs=(
            P("dp", "tensor", None),
            P("dp", "tensor", None),
            P("dp"),
            P("dp", "tensor"),
            P("dp", None),
            P("tensor", "dp"),
            P("dp"),
            P("dp", "tensor"),
            P("dp", "tensor"),
            P("tensor", "dp"),
            P(),
            P(),
        ),
        check_vma=False,
    )
```

```python
from functools import partial

import jax
import jax.numpy as jnp
import numpy as np
from jax import lax
from jax.experimental import pallas as pl
from jax.experimental.pallas import tpu as pltpu
from jax.sharding import PartitionSpec as P

norm_eps = 1e-06
rope_base = 10000.0
masked_score = -1e30
f32 = jnp.float32
bf16 = jnp.bfloat16

RING = (0, 2, 4, 6, 7, 5, 3, 1)
OFFSETS = (0, -1, 1, -2, 2, -3, 3, 4)
PLACE = {ring: slot for slot, ring in enumerate(OFFSETS)}
vmem_bytes = 48 * 1024 * 1024


def nn(left, right):
    return lax.dot_general(left, right, (((1,), (0,)), ((), ())), preferred_element_type=f32)


def nt(left, right):
    return lax.dot_general(left, right, (((1,), (1,)), ((), ())), preferred_element_type=f32)


def tn(left, right):
    return lax.dot_general(left, right, (((0,), (0,)), ((), ())), preferred_element_type=f32)


def ringed():
    return lax.axis_size("dp") == len(RING)


def owner_tables():
    size = len(RING)
    owners = np.zeros((size, size), np.int32)
    for index in range(size):
        spot = RING.index(index)
        for slot, offset in enumerate(OFFSETS):
            owners[index, slot] = RING[(spot + offset) % size]
    return owners


def call(kernel, outs, ins, smem=0, flops=0):
    single = not isinstance(outs, (list, tuple))
    return pl.pallas_call(
        kernel,
        out_shape=outs if single else tuple(outs),
        in_specs=[
            pl.BlockSpec(memory_space=pltpu.SMEM if i < smem else pltpu.VMEM)
            for i in range(len(ins))
        ],
        out_specs=(
            pl.BlockSpec(memory_space=pltpu.VMEM)
            if single
            else tuple(pl.BlockSpec(memory_space=pltpu.VMEM) for _ in outs)
        ),
        compiler_params=pltpu.CompilerParams(vmem_limit_bytes=vmem_bytes),
        cost_estimate=pl.CostEstimate(flops=flops, bytes_accessed=8_000_000, transcendentals=0),
    )(*ins)


def to_ring_kernel(owners, *refs):
    count = len(refs) // 2
    width = refs[0].shape[1] // len(RING)
    for source, target in zip(refs[:count], refs[count:]):
        for slot in range(len(RING)):
            begin = pl.multiple_of(owners[slot] * width, width)
            target[:, slot * width : (slot + 1) * width] = source[:, pl.ds(begin, width)]


def from_ring_kernel(owners, *refs):
    count = len(refs) // 2
    width = refs[0].shape[1] // len(RING)
    for source, target in zip(refs[:count], refs[count:]):
        for slot in range(len(RING)):
            begin = pl.multiple_of(owners[slot] * width, width)
            target[:, pl.ds(begin, width)] = source[:, slot * width : (slot + 1) * width]


def reorder(kernel, *arrays):
    if not ringed():
        return arrays
    owners = jnp.asarray(owner_tables())[lax.axis_index("dp")]
    shapes = [jax.ShapeDtypeStruct(array.shape, array.dtype) for array in arrays]
    return call(kernel, shapes, (owners, *arrays), smem=1)


def step(rows, forward):
    size = len(RING)
    move = 1 if forward else -1
    return lax.ppermute(
        rows, "dp", [(RING[i], RING[(i + move) % size]) for i in range(size)]
    )


def join(pieces, sizes):
    width = pieces[0][2].shape[1]
    ends = np.cumsum(sizes).tolist()
    places = []
    for row, slot, block in pieces:
        cuts = []
        for i, (end, size) in enumerate(zip(ends, sizes)):
            low = max(row, end - size)
            high = min(row + block.shape[0], end)
            if low < high:
                cuts.append((i, low - end + size, slot * width, low - row, high - low))
        places.append(cuts)

    count = sum(len(cuts) for cuts in places)

    def kernel(*refs):
        blocks, wholes, signals = refs[: len(pieces)], refs[len(pieces) : -1], refs[-1]
        copies = []
        for block, cuts in zip(blocks, places):
            for i, low, column, begin, size in cuts:
                copies.append(
                    pltpu.make_async_copy(
                        block.at[begin : begin + size],
                        wholes[i].at[low : low + size, column : column + width],
                        signals.at[len(copies)],
                    )
                )
        for copy in copies:
            copy.start()
        for copy in copies:
            copy.wait()

    return pl.pallas_call(
        kernel,
        out_shape=[
            jax.ShapeDtypeStruct((size, width * len(RING)), pieces[0][2].dtype)
            for size in sizes
        ],
        in_specs=[pl.BlockSpec(memory_space=pltpu.HBM) for _ in pieces],
        out_specs=[pl.BlockSpec(memory_space=pltpu.VMEM) for _ in sizes],
        scratch_shapes=[pltpu.SemaphoreType.DMA((count,))],
        compiler_params=pltpu.CompilerParams(vmem_limit_bytes=vmem_bytes),
        cost_estimate=pl.CostEstimate(flops=0, bytes_accessed=8_000_000, transcendentals=0),
    )(*[block for _, _, block in pieces])


def gather_steps(shard, far):
    pieces = [(0, PLACE[0], shard)]
    ahead = behind = shard
    for hop in (1, 2, 3):
        ahead, behind = yield [(ahead, True), (behind, False)]
        pieces += [(0, PLACE[-hop], ahead), (0, PLACE[hop], behind)]
    if far == "both":
        half = shard.shape[0] // 2
        first, second = yield [(ahead[:half], True), (behind[half:], False)]
        pieces += [(0, PLACE[4], first), (half, PLACE[4], second)]
    else:
        (last,) = yield [(ahead, True) if far == "ahead" else (behind, False)]
        pieces.append((0, PLACE[4], last))
    return pieces


def reduce_steps(grads, far, order):
    width = grads[0].shape[1] // len(RING)
    half = sum(grad.shape[0] for grad in grads) // 2

    def part(offset, *bounds):
        slot = PLACE[offset]
        cut = [grad[:, slot * width : (slot + 1) * width] for grad in grads]
        whole = cut[0] if len(cut) == 1 else jnp.concatenate(cut, axis=0)
        return whole.astype(f32)

    last = order.leave(part(4).astype(bf16))
    if far == "both":
        got = yield [(last[:half], True), (last[half:], False)]
        first, second = order(*got)
        ahead, behind = part(3), part(-3)
        ahead = jnp.concatenate([ahead[:half] + first, ahead[half:]], axis=0)
        behind = jnp.concatenate([behind[:half], behind[half:] + second], axis=0)
    elif far == "ahead":
        (got,) = yield [(last, True)]
        ahead, behind = part(3) + order(got), part(-3)
    else:
        (got,) = yield [(last, False)]
        ahead, behind = part(3), part(-3) + order(got)
    for hop in (2, 1, 0):
        ahead, behind = order.leave(ahead.astype(bf16), behind.astype(bf16))
        got = yield [(ahead, True), (behind, False)]
        ahead, behind = order(*got)
        if hop:
            ahead = part(hop) + ahead
            behind = part(-hop) + behind
    return order.leave(part(0) + ahead + behind)


class Order:
    def __init__(self):
        self.last = ()

    def __call__(self, *values):
        out = lax.optimization_barrier((*values, *self.last))[: len(values)]
        return out if len(out) > 1 else out[0]

    def leave(self, *values):
        self.last = values
        return values if len(values) > 1 else values[0]


class Links:
    def __init__(self, order, depth):
        self.order = order
        self.depth = depth
        self.done = []
        self.plans = {}
        self.got = {}
        self.results = {}

    def gather(self, name, shard, far):
        if ringed():
            self.plans[name] = gather_steps(shard, far)
            self.got[name] = None
        else:
            self.results[name] = lax.all_gather(shard, "dp", axis=1, tiled=True)

    def whole(self, names, sizes):
        got = [self.finish(name) for name in names]
        if not ringed():
            rows = jnp.concatenate(got, axis=0)
            ends = np.cumsum(sizes).tolist()
            return [rows[end - size : end] for end, size in zip(ends, sizes)]
        pieces = []
        base = 0
        for some in got:
            pieces += [(base + row, slot, block) for row, slot, block in some]
            base += some[0][2].shape[0]
        blocks = self.order(*[block for _, _, block in pieces])
        pieces = [(row, slot, block) for (row, slot, _), block in zip(pieces, blocks)]
        out = join(pieces, sizes)
        self.order.leave(*out)
        return out

    def reduce(self, name, grads, far):
        if ringed():
            self.plans[name] = reduce_steps(grads, far, self.order)
            self.got[name] = None
        else:
            self.results[name] = lax.psum_scatter(
                jnp.concatenate(grads, axis=0), "dp", scatter_dimension=1, tiled=True
            ).astype(f32)

    def go(self, names):
        if not ringed():
            return
        held = self.done[-self.depth] if len(self.done) >= self.depth else []
        sends = [(name, *send) for name in names.split() for send in self.plans[name].send(self.got[name])]
        rows = lax.optimization_barrier((*[send[1] for send in sends], *held, *self.order.last))
        self.order.leave(*rows[: len(sends)])
        arrived = []
        for name in names.split():
            self.got[name] = []
        for row, (name, _, forward) in zip(rows, sends):
            with jax.named_scope(name):
                got = step(row, forward)
            self.got[name].append(got)
            arrived.append(got)
        self.done.append(arrived)

    def finish(self, name):
        if ringed():
            try:
                self.plans[name].send(self.got[name])
            except StopIteration as stop:
                return stop.value
        return self.results[name]


def swap(rows, bit, axis="tensor"):
    count = lax.axis_size(axis)
    return lax.ppermute(rows, axis, [(i, i ^ bit) for i in range(count)])


BLOCKS = (0, 2, 1, 3)


class Collect:
    def __init__(self, order, rows):
        self.order = order
        self.own = order(rows)
        self.across = swap(self.own, 2)
        self.core = swap(self.own, 1)
        order.leave(self.own)

    def middle(self):
        self.across = self.order.leave(self.order(self.across))
        self.corner = swap(self.across, 1)

    def end(self):
        return self.order(self.own, self.across, self.core, self.corner)


class Spread:
    def __init__(self, order, product, count):
        self.order = order
        self.count = count
        far = order.leave(product(slice(2 * count, None)).astype(bf16))
        self.core = swap(far, 1)
        self.near = order.leave(product(slice(0, 2 * count)).astype(bf16))

    def middle(self):
        self.core, near = self.order(self.core, self.near)
        sent = near[self.count :].astype(f32) + self.core[self.count :].astype(f32)
        sent = self.order.leave(sent.astype(bf16))
        self.across = swap(sent, 2)

    def end(self):
        near, core, across = self.order(self.near, self.core, self.across)
        kept = near[: self.count].astype(f32) + core[: self.count].astype(f32)
        return kept + across.astype(f32)


def turn(values):
    half = values.shape[0] // 2
    return jnp.concatenate([-values[half:], values[:half]], axis=0)


def turn_back(values):
    half = values.shape[0] // 2
    return jnp.concatenate([values[half:], -values[:half]], axis=0)


def head_scale(pre):
    return lax.rsqrt(jnp.mean(pre * pre, axis=0, keepdims=True) + norm_eps)


def head_prep(pre, gain, cosine, sine):
    scaled = pre * head_scale(pre) * gain
    return scaled * cosine + turn(scaled) * sine


def head_back(grad, pre, gain, cosine, sine):
    grad = grad * cosine + turn_back(grad * sine)
    scale = head_scale(pre)
    lifted = grad * gain
    back = scale * lifted - pre * (scale**3) * jnp.mean(lifted * pre, axis=0, keepdims=True)
    return back, grad * pre * scale


def pick(which, options):
    out = options[0]
    for i in range(1, len(options)):
        out = jnp.where(which == i, options[i], out)
    return out


def put(target, rows, s, seqs, block):
    part = block.shape[1] // len(BLOCKS)
    for i in range(len(BLOCKS)):
        begin = (i * seqs + s) * part
        target[rows, begin : begin + part] = block[:, i * part : (i + 1) * part]


def get(source, rows, s, seqs):
    part = source.shape[1] // (len(BLOCKS) * seqs)
    begins = [(i * seqs + s) * part for i in range(len(BLOCKS))]
    return jnp.concatenate([source[rows, begin : begin + part] for begin in begins], axis=1)


def attend_kernel(
    heads, kv_local, seqs, kv_of, qkv, q_gain, k_gain, cosine, sine, at_row, at_col,
    mixed, queries, keys, values, log_total,
):
    head = q_gain.shape[0]
    span = cosine.shape[1]
    causal = at_row[...] >= at_col[...]
    k_base = heads * head
    v_base = k_base + kv_local * head
    for s in range(seqs):
        lanes = slice(s * span, (s + 1) * span)
        key_list = []
        value_list = []
        for c in range(kv_local):
            rows = slice(c * head, (c + 1) * head)
            key = head_prep(
                qkv[k_base + c * head : k_base + (c + 1) * head, lanes],
                k_gain[...], cosine[...], sine[...],
            ).astype(bf16)
            value = qkv[v_base + c * head : v_base + (c + 1) * head, lanes].astype(bf16)
            keys[rows, lanes] = key
            values[rows, lanes] = value
            key_list.append(key)
            value_list.append(value)
        for h in range(heads):
            rows = slice(h * head, (h + 1) * head)
            query = head_prep(qkv[rows, lanes], q_gain[...], cosine[...], sine[...]).astype(bf16)
            queries[rows, lanes] = query
            key = pick(kv_of[h], key_list)
            value = pick(kv_of[h], value_list)
            scores = jnp.where(causal, tn(key, query) * head ** (-0.5), masked_score)
            top = jnp.max(scores, axis=0, keepdims=True)
            expos = jnp.exp(scores - top)
            total = jnp.sum(expos, axis=0, keepdims=True)
            log_total[h : h + 1, lanes] = top + jnp.log(total)
            probs = (expos / total).astype(bf16)
            put(mixed, rows, s, seqs, nn(value, probs).astype(bf16))


def attend_back_kernel(
    heads, kv_local, seqs, kv_of, grad_mixed, qkv, queries, keys, values, log_total,
    q_gain, k_gain, cosine, sine, at_row, at_col, row_scale,
    grad_qkv, grad_blocks, gain_grads,
):
    head = q_gain.shape[0]
    span = cosine.shape[1]
    causal = at_row[...] >= at_col[...]
    k_base = heads * head
    v_base = k_base + kv_local * head
    factor = head ** (-0.5)
    q_sum = jnp.zeros((head, span), f32)
    k_sum = jnp.zeros((head, span), f32)
    for s in range(seqs):
        lanes = slice(s * span, (s + 1) * span)
        scale = row_scale[:, lanes]
        kv_rows = [slice(c * head, (c + 1) * head) for c in range(kv_local)]
        key_list = [keys[rows, lanes] for rows in kv_rows]
        value_list = [values[rows, lanes] for rows in kv_rows]
        grad_keys = [jnp.zeros((head, span), f32) for _ in kv_rows]
        grad_values = [jnp.zeros((head, span), f32) for _ in kv_rows]
        for h in range(heads):
            rows = slice(h * head, (h + 1) * head)
            query = queries[rows, lanes]
            grad = get(grad_mixed, rows, s, seqs)
            key = pick(kv_of[h], key_list)
            value = pick(kv_of[h], value_list)
            scores = jnp.where(causal, tn(key, query) * factor, masked_score)
            soft = jnp.exp(scores - log_total[h : h + 1, lanes])
            grad_probs = tn(value, grad)
            inner = jnp.sum(soft * grad_probs, axis=0, keepdims=True)
            grad_scores = (soft * (grad_probs - inner)).astype(bf16)
            grad_query = nn(key, grad_scores) * factor
            grad_key = nt(query, grad_scores) * factor
            grad_value = nt(grad, soft.astype(bf16))
            for c in range(kv_local):
                mine = kv_of[h] == c
                grad_keys[c] = grad_keys[c] + jnp.where(mine, grad_key, 0.0)
                grad_values[c] = grad_values[c] + jnp.where(mine, grad_value, 0.0)
            back, gain = head_back(
                grad_query, qkv[rows, lanes], q_gain[...], cosine[...], sine[...]
            )
            q_sum = q_sum + gain
            back = (back * scale).astype(bf16)
            grad_qkv[rows, lanes] = back
            put(grad_blocks, rows, s, seqs, back)
        for c in range(kv_local):
            rows = slice(k_base + c * head, k_base + (c + 1) * head)
            back, gain = head_back(
                grad_keys[c], qkv[rows, lanes], k_gain[...], cosine[...], sine[...]
            )
            k_sum = k_sum + gain
            back = (back * scale).astype(bf16)
            grad_qkv[rows, lanes] = back
            put(grad_blocks, rows, s, seqs, back)
            rows = slice(v_base + c * head, v_base + (c + 1) * head)
            back = (grad_values[c] * scale).astype(bf16)
            grad_qkv[rows, lanes] = back
            put(grad_blocks, rows, s, seqs, back)
    gain_grads[:head] = jnp.sum(q_sum, axis=1, keepdims=True)
    gain_grads[head:] = jnp.sum(k_sum, axis=1, keepdims=True)


def local(
    inputs,
    attn_norm,
    query_weight,
    key_value_weight,
    out_weight,
    ffn_norm,
    gate_weight,
    up_weight,
    down_weight,
    query_gain,
    key_gain,
    cotangent,
):
    ranks = lax.axis_size("tensor")
    rank = lax.axis_index("tensor")
    seqs, span, width = inputs.shape
    head = query_gain.shape[0]
    heads = query_weight.shape[1] // head
    kv_heads = key_value_weight.shape[1] // (2 * head)
    group = heads * ranks // kv_heads
    kv_first = [(i * heads) // group for i in range(ranks)]
    kv_last = [(i * heads + heads - 1) // group for i in range(ranks)]
    kv_local = max(b - a for a, b in zip(kv_first, kv_last)) + 1
    kv_start = jnp.asarray(
        np.asarray([min(a, kv_heads - kv_local) for a in kv_first], np.int32)
    )[rank]
    kv_of = (rank * heads + jnp.arange(heads, dtype=jnp.int32)) // group - kv_start
    rows = seqs * span
    units = gate_weight.shape[1]
    q_cols = heads * head
    kv_cols = kv_local * head
    seq_len = ranks * span

    order = Order()
    links = Links(order, 2)
    links.gather("down", down_weight, "both")
    links.go("down")

    attn_gain = attn_norm.astype(f32)
    ffn_gain = ffn_norm.astype(f32)
    query_weight, key_value_weight = order(query_weight, key_value_weight)
    key_weight = lax.dynamic_slice_in_dim(key_value_weight, kv_start * head, kv_cols, axis=1)
    value_weight = lax.dynamic_slice_in_dim(
        key_value_weight, (kv_heads + kv_start) * head, kv_cols, axis=1
    )
    qkv_own = jnp.concatenate([query_weight.T, key_weight.T, value_weight.T], axis=0)
    qkv_rows = qkv_own.shape[0]
    cut = (q_cols + qkv_rows) // 2
    qkv_shard = (qkv_own.astype(f32) * attn_gain[None]).astype(bf16)
    shard_a = qkv_shard[:cut]
    shard_b = jnp.concatenate([qkv_shard[cut:], out_weight])
    order.leave(shard_a, shard_b)
    links.gather("attn_a", shard_a, "ahead")
    links.gather("attn_b", shard_b, "behind")
    links.go("attn_a")
    tokens_low, cot_low = reorder(
        to_ring_kernel, *order(inputs.reshape(rows, width), cotangent.reshape(rows, width))
    )
    order.leave(tokens_low, cot_low)
    tokens = tokens_low.astype(f32)
    gather_x = Collect(order, tokens_low)
    links.go("attn_b")
    gate_own, up_own = order(gate_weight.T, up_weight.T)
    gate_shard = (gate_own.astype(f32) * ffn_gain[None]).astype(bf16)
    up_shard = (up_own.astype(f32) * ffn_gain[None]).astype(bf16)
    order.leave(gate_shard, up_shard)
    links.gather("gate", gate_shard, "ahead")
    links.gather("up", up_shard, "behind")
    links.go("attn_a")

    block_of = rank ^ jnp.asarray(BLOCKS, jnp.int32)
    positions = (block_of[:, None] * span + jnp.arange(span, dtype=jnp.int32)[None]).reshape(-1)
    inverse = rope_base ** (-2.0 * jnp.arange(head // 2, dtype=f32) / head)
    angles = inverse[:, None] * positions.astype(f32)[None]
    cosine = jnp.concatenate([jnp.cos(angles)] * 2, axis=0)
    sine = jnp.concatenate([jnp.sin(angles)] * 2, axis=0)
    tables = (
        query_gain.astype(f32)[:, None],
        key_gain.astype(f32)[:, None],
        cosine,
        sine,
        positions[None, :],
        positions[:, None],
    )

    links.go("attn_b")
    gather_x.middle()
    gather_cot = Collect(order, cot_low)
    links.go("attn_a")
    parts = [part.reshape(inputs.shape) for part in gather_x.end()]
    whole = jnp.concatenate(parts, axis=1).reshape(seqs * seq_len, width)
    wide = whole.astype(f32)
    row_scale = lax.rsqrt(jnp.mean(wide * wide, axis=-1) + norm_eps)[None]
    order.leave(whole, row_scale)
    links.go("attn_b")
    links.go("attn_a attn_b")
    gather_cot.middle()
    links.go("gate")
    qkv_full, out_full = links.whole(["attn_a", "attn_b"], [qkv_rows, q_cols])
    links.go("up")
    qkv = nt(qkv_full, whole) * row_scale
    order.leave(qkv)
    links.go("down")

    def column(count, kind):
        return jax.ShapeDtypeStruct((count, seqs * seq_len), kind)

    mixed, queries, keys, values, log_total = call(
        partial(attend_kernel, heads, kv_local, seqs),
        (column(q_cols, bf16), column(q_cols, bf16), column(kv_cols, bf16),
         column(kv_cols, bf16), column(heads, f32)),
        (kv_of, order(qkv), *tables),
        smem=1,
    )
    order.leave(mixed)
    links.go("gate")
    attn_sum = Spread(order, lambda part: tn(mixed[:, part], out_full), rows)
    links.go("up")
    attn_sum.middle()
    links.go("down")
    cot_whole = order.leave(jnp.concatenate(gather_cot.end(), axis=0))
    links.go("gate")
    middle = tokens + attn_sum.end()
    mid_scale = lax.rsqrt(jnp.mean(middle * middle, axis=-1, keepdims=True) + norm_eps)
    normed_low = (middle * mid_scale).astype(bf16)
    order.leave(normed_low, middle)
    gather_ffn = Collect(order, normed_low)
    links.go("up")
    links.go("gate up")
    gather_ffn.middle()
    links.go("down")
    ffn_whole = order.leave(jnp.concatenate(gather_ffn.end(), axis=0))
    (gate_full,) = links.whole(["gate"], [units])
    (up_full,) = links.whole(["up"], [units])
    ffn_whole = order(ffn_whole)
    gate = nt(gate_full, ffn_whole)
    upward = nt(up_full, ffn_whole)
    hidden = (gate * jax.nn.sigmoid(gate) * upward).astype(bf16)
    hidden, gate, upward = order.leave(*lax.optimization_barrier((hidden, gate, upward)))
    down_part = order.leave(nn(hidden, order(cot_whole)).astype(bf16))
    links.reduce("down_sum", [down_part], "both")
    links.go("down_sum")
    (down_full,) = links.whole(["down"], [units])
    grad_hidden = nt(down_full, cot_whole)
    sig = jax.nn.sigmoid(gate)
    grad_gate = (grad_hidden * upward * sig * (1.0 + gate * (1.0 - sig))).astype(bf16)
    grad_up = (grad_hidden * (gate * sig)).astype(bf16)
    order.leave(grad_gate, grad_up)
    ffn_sum = Spread(
        order,
        lambda part: tn(grad_gate[:, part], gate_full) + tn(grad_up[:, part], up_full),
        rows,
    )
    links.go("down_sum")
    ffn_sum.middle()
    gate_part, up_part = order(grad_gate, grad_up)
    gate_part = nn(gate_part, ffn_whole).astype(bf16)
    up_part = nn(up_part, ffn_whole).astype(bf16)
    order.leave(gate_part, up_part)
    links.reduce("gate_sum", [gate_part], "behind")
    links.reduce("up_sum", [up_part], "ahead")
    links.go("gate_sum up_sum")
    links.go("down_sum")
    lifted = ffn_sum.end()
    grad_middle = (
        cot_low.astype(f32)
        + mid_scale * lifted
        - middle * mid_scale**3 * jnp.mean(lifted * middle, axis=-1, keepdims=True)
    )
    grad_low = grad_middle.astype(bf16)
    order.leave(grad_low, grad_middle)
    gather_grad = Collect(order, grad_low)
    links.go("gate_sum")
    result_sum = Spread(order, lambda part: tn(order(hidden)[:, part], down_full), rows)
    links.go("up_sum")
    gather_grad.middle()
    links.go("gate_sum")
    grad_attn = jnp.concatenate(gather_grad.end(), axis=0)
    grad_mixed = order.leave(nt(out_full, grad_attn).astype(bf16))
    grad_qkv, grad_blocks, gains = call(
        partial(attend_back_kernel, heads, kv_local, seqs),
        (column(qkv_rows, bf16), column(qkv_rows, bf16),
         jax.ShapeDtypeStruct((2 * head, 1), f32)),
        (kv_of, grad_mixed, qkv, queries, keys, values, log_total, *tables, row_scale),
        smem=1,
    )
    order.leave(grad_qkv, grad_blocks, gains)
    links.go("up_sum")
    result_sum.middle()
    qkv_part = nn(order(grad_qkv), whole).astype(bf16)
    out_part = nn(mixed, grad_attn).astype(bf16)
    order.leave(qkv_part, out_part)
    links.reduce("attn_a_sum", [qkv_part[:cut]], "ahead")
    links.reduce("attn_b_sum", [qkv_part[cut:], out_part], "behind")
    links.go("attn_a_sum attn_b_sum")
    gains = gains.reshape(1, 2 * head)
    gains_step = swap(gains, 1, "dp")
    input_sum = Spread(order, lambda part: tn(grad_blocks[:, part], qkv_full), rows)
    links.go("gate_sum")
    input_sum.middle()
    (result,) = reorder(from_ring_kernel, (middle + result_sum.end()).astype(bf16))
    order.leave(result)
    links.go("attn_a_sum")
    links.go("attn_b_sum")
    bits = [1 << i for i in range(1, lax.axis_size("dp").bit_length() - 1)]
    for bit in bits[:1]:
        gains = order.leave(gains + order(gains_step))
        gains_step = swap(gains, bit, "dp")
    gate_grad = links.finish("gate_sum")
    gate_out = (gate_grad * ffn_gain[None]).T
    gate_norm = jnp.sum(gate_grad * gate_own.astype(f32), axis=0)
    order.leave(gate_out, gate_norm)
    links.go("up_sum")
    links.go("attn_a_sum")
    links.go("attn_b_sum")
    for bit in bits[1:]:
        gains = order.leave(gains + order(gains_step))
        gains_step = swap(gains, bit, "dp")
    lifted = input_sum.end()
    own_scale = lax.rsqrt(jnp.mean(tokens * tokens, axis=-1, keepdims=True) + norm_eps)
    input_grad = grad_middle + lifted - tokens * own_scale**2 * jnp.mean(
        lifted * tokens, axis=-1, keepdims=True
    )
    (input_grad,) = reorder(from_ring_kernel, input_grad)
    order.leave(input_grad)
    links.go("attn_a_sum")
    links.go("attn_b_sum")
    up_grad = links.finish("up_sum")
    up_out = (up_grad * ffn_gain[None]).T
    ffn_norm_grad = gate_norm + jnp.sum(up_grad * up_own.astype(f32), axis=0)
    order.leave(up_out, ffn_norm_grad)
    links.go("down_sum")
    gains = order.leave(gains + order(gains_step))
    attn_grad = jnp.concatenate([links.finish("attn_a_sum"), links.finish("attn_b_sum")], axis=0)
    qkv_grad = attn_grad[:qkv_rows]
    out_grad = attn_grad[qkv_rows:]

    attn_norm_grad = jnp.sum(qkv_grad * qkv_own.astype(f32), axis=0)
    slab = attn_norm_grad.shape[0]
    qkv_grad = qkv_grad * attn_gain[None]
    small = jnp.concatenate([attn_norm_grad, ffn_norm_grad, gains[0]])[None]
    own = qkv_grad[q_cols:].astype(bf16)
    across = swap(own, 2)
    core = swap(own, 1)
    small = small + swap(small, 1)
    small = small + swap(small, 2)
    corner = swap(across, 1)
    by_bits = jnp.stack([own, core, across, corner])
    by_rank = [
        lax.dynamic_index_in_dim(by_bits, rank ^ i, keepdims=False).reshape(
            2, kv_local, head, slab
        )
        for i in range(ranks)
    ]
    kv_sum = []
    for kind in range(2):
        for c in range(kv_heads):
            total = jnp.zeros((head, slab), f32)
            for i in range(ranks):
                spot = c - min(kv_first[i], kv_heads - kv_local)
                if 0 <= spot < kv_local:
                    total = total + by_rank[i][kind, spot].astype(f32)
            kv_sum.append(total)
    down_grad = links.finish("down_sum")
    return (
        result.reshape(inputs.shape),
        input_grad.reshape(inputs.shape),
        small[0, :slab],
        qkv_grad[:q_cols].T,
        jnp.concatenate(kv_sum, axis=0).T,
        out_grad,
        small[0, slab : 2 * slab],
        gate_out,
        up_out,
        down_grad,
        small[0, 2 * slab : 2 * slab + head],
        small[0, 2 * slab + head :],
    )


def solution(mesh):
    placed = (
        P("dp", "tensor", None),
        P("dp"),
        P("dp", "tensor"),
        P("dp", None),
        P("tensor", "dp"),
        P("dp"),
        P("dp", "tensor"),
        P("dp", "tensor"),
        P("tensor", "dp"),
        P(),
        P(),
        P("dp", "tensor", None),
    )
    return jax.shard_map(
        local,
        mesh=mesh,
        in_specs=placed,
        out_specs=(
            P("dp", "tensor", None),
            P("dp", "tensor", None),
            P("dp"),
            P("dp", "tensor"),
            P("dp", None),
            P("tensor", "dp"),
            P("dp"),
            P("dp", "tensor"),
            P("dp", "tensor"),
            P("tensor", "dp"),
            P(),
            P(),
        ),
        check_vma=False,
    )
```

```python
from functools import partial
from types import SimpleNamespace

import jax
import jax.numpy as jnp
import numpy as np
from jax import lax
from jax.experimental import pallas as pl
from jax.experimental.pallas import tpu as pltpu
from jax.sharding import PartitionSpec as P

norm_eps = 1e-06
rope_base = 10000.0
masked_score = -1e30
f32 = jnp.float32
bf16 = jnp.bfloat16
big_vmem = 60 * 1024 * 1024
small_vmem = 12 * 1024 * 1024

RING = (0, 2, 4, 6, 7, 5, 3, 1)
OFFSETS = (0, -1, 1, -2, 2, -3, 3, 4)
PLACE = {ring: slot for slot, ring in enumerate(OFFSETS)}
BLOCKS = (0, 2, 1, 3)


class Ring:
    down, attn_a, attn_b, gate, up = range(5)
    down_sum, attn_a_sum, attn_b_sum, gate_sum, up_sum = range(5, 10)


def nn(left, right):
    return lax.dot_general(left, right, (((1,), (0,)), ((), ())), preferred_element_type=f32)


def nt(left, right, precision=None):
    return lax.dot_general(
        left, right, (((1,), (1,)), ((), ())), precision=precision, preferred_element_type=f32
    )


def tn(left, right):
    return lax.dot_general(left, right, (((0,), (0,)), ((), ())), preferred_element_type=f32)


def ringed():
    return lax.axis_size("dp") == len(RING)


def slots():
    return len(RING) if ringed() else 1


def owners():
    if not ringed():
        return jnp.zeros((1,), jnp.int32)
    table = np.zeros((len(RING), len(RING)), np.int32)
    for spot, index in enumerate(RING):
        for slot, offset in enumerate(OFFSETS):
            table[index, slot] = RING[(spot + offset) % len(RING)]
    return jnp.asarray(table)[lax.axis_index("dp")]


def shaped(*shape, kind=bf16):
    return jax.ShapeDtypeStruct(shape, kind)


def call(body, outs, smem=(), vmem=(), loads=(), direct=(), grant=None):
    arrays = []
    index = {}
    plans = []
    for shape, cuts in loads:
        plan = []
        for row, column, first, count, array in cuts:
            if id(array) not in index:
                index[id(array)] = len(arrays)
                arrays.append(array)
            plan.append((row, column, first, count, index[id(array)]))
        plans.append((shape, plan))
    copies = sum(len(plan) for _, plan in plans)

    def kernel(*refs):
        refs = list(refs)
        scalars = [refs.pop(0) for _ in smem]
        blocks = [refs.pop(0) for _ in vmem]
        sources = [refs.pop(0) for _ in arrays]
        finals = [refs.pop(0) for _ in outs]
        targets = list(finals)
        for place in direct:
            targets[place] = refs.pop(0)
        getters = []
        number = 0
        for (_, plan), scratch in zip(plans, refs):
            mine = []
            for row, column, first, count, source in plan:
                width = sources[source].shape[1]
                copy = pltpu.make_async_copy(
                    sources[source].at[pl.ds(first, count)],
                    scratch.at[pl.ds(row, count), pl.ds(column, width)],
                    refs[-1].at[number],
                )
                copy.start()
                mine.append(copy)
                number += 1

            def getter(mine=mine, scratch=scratch):
                for copy in mine:
                    copy.wait()
                return scratch

            getters.append(getter)
        body(*scalars, *blocks, *getters, *targets)
        ends = []
        for place in direct:
            copy = pltpu.make_async_copy(targets[place], finals[place], refs[-1].at[number])
            copy.start()
            ends.append(copy)
            number += 1
        for copy in ends:
            copy.wait()

    scratch = [pltpu.VMEM(outs[place].shape, outs[place].dtype) for place in direct]
    scratch += [pltpu.VMEM(shape, bf16) for shape, _ in plans]
    if scratch:
        scratch.append(pltpu.SemaphoreType.DMA((copies + len(direct),)))
    return pl.pallas_call(
        kernel,
        out_shape=tuple(outs),
        in_specs=[pl.BlockSpec(memory_space=pltpu.SMEM) for _ in smem]
        + [pl.BlockSpec(memory_space=pltpu.VMEM) for _ in vmem]
        + [pl.BlockSpec(memory_space=pl.ANY) for _ in arrays],
        out_specs=tuple(
            pl.BlockSpec(memory_space=pltpu.HBM if i in direct else pltpu.VMEM)
            for i in range(len(outs))
        ),
        scratch_shapes=scratch,
        compiler_params=pltpu.CompilerParams(vmem_limit_bytes=grant or (big_vmem if loads else small_vmem)),
        cost_estimate=pl.CostEstimate(flops=0, bytes_accessed=0, transcendentals=0),
    )(*smem, *vmem, *arrays)


class Order:
    def __init__(self):
        self.last = ()

    def __call__(self, *values):
        out = lax.optimization_barrier((*values, *self.last))[: len(values)]
        return out if len(out) > 1 else out[0]

    def wait(self, *values):
        out = self(*values)
        return self.leave(*out) if len(values) > 1 else self.leave(out)

    def leave(self, *values):
        self.last = values
        return values if len(values) > 1 else values[0]

    def call(self, body, outs, smem=(), vmem=(), loads=(), direct=(), grant=None):
        arrays = [*vmem, *(cut[4] for _, cuts in loads for cut in cuts)]
        held = lax.optimization_barrier((*arrays, *self.last))
        vmem = held[: len(vmem)]
        left = list(held[len(vmem) : len(arrays)])
        seen = {}
        new = []
        for shape, cuts in loads:
            made = []
            for row, column, first, count, array in cuts:
                same = seen.setdefault(id(array), left.pop(0))
                made.append((row, column, first, count, same))
            new.append((shape, made))
        return self.leave(*call(body, outs, smem, vmem, new, direct, grant))


def load_ring(source, owner, target):
    count = slots()
    width = source.shape[1] // count
    for slot in range(count):
        begin = pl.multiple_of(owner[slot] * width, width)
        target[:, slot * width : (slot + 1) * width] = source[:, pl.ds(begin, width)]


def store_ring(target, owner, values):
    count = slots()
    width = target.shape[1] // count
    for slot in range(count):
        begin = pl.multiple_of(owner[slot] * width, width)
        target[:, pl.ds(begin, width)] = values[:, slot * width : (slot + 1) * width]


def step(rows, forward):
    size = len(RING)
    move = 1 if forward else -1
    return lax.ppermute(
        rows, "dp", [(RING[i], RING[(i + move) % size]) for i in range(size)]
    )


def swap(rows, bit, axis="tensor"):
    count = lax.axis_size(axis)
    return lax.ppermute(rows, axis, [(i, i ^ bit) for i in range(count)])


def gather_steps(shard, far):
    pieces = [(PLACE[0], shard)]
    ahead = behind = shard
    for hop in (1, 2, 3):
        ahead, behind = yield [(ahead, True), (behind, False)]
        pieces += [(PLACE[-hop], ahead), (PLACE[hop], behind)]
    (last,) = yield [(ahead, True) if far == "ahead" else (behind, False)]
    pieces.append((PLACE[4], last))
    return pieces


def add_body(*refs):
    count = len(refs) // 3
    for i in range(count):
        total = refs[2 * i][...].astype(f32) + refs[2 * i + 1][...].astype(f32)
        refs[2 * count + i][...] = total.astype(bf16)


def reduce_steps(parts, far, order):
    shape = shaped(*parts[0].shape)

    def part(offset):
        return parts[PLACE[offset]]

    (got,) = yield [(part(4), far == "ahead")]
    ahead, behind = part(3), part(-3)
    if far == "ahead":
        ahead = order.call(add_body, [shape], vmem=(got, ahead))
    else:
        behind = order.call(add_body, [shape], vmem=(got, behind))
    for hop in (2, 1, 0):
        got = yield [(ahead, True), (behind, False)]
        if hop:
            ahead, behind = order.call(
                add_body, [shape] * 2, vmem=(got[0], part(hop), got[1], part(-hop))
            )
    return part(0), *got


class Links:
    def __init__(self, order):
        self.order = order
        self.done = []
        self.plans = {}
        self.got = {}
        self.results = {}

    def gather(self, name, shard, far):
        if ringed():
            self.plans[name] = gather_steps(shard, far)
            self.got[name] = None
        else:
            self.results[name] = [(0, lax.all_gather(shard, "dp", axis=1, tiled=True))]

    def reduce(self, name, parts, far):
        if ringed():
            self.plans[name] = reduce_steps(parts, far, self.order)
            self.got[name] = None
        else:
            total = lax.psum_scatter(parts[0], "dp", scatter_dimension=1, tiled=True)
            self.results[name] = [total]

    def go(self, names, depth=2):
        if not ringed():
            return
        sends = [
            (name, *send) for name in names for send in self.plans[name].send(self.got[name])
        ]
        held = self.done[-depth] if len(self.done) >= depth else []
        rows = self.order(*[send[1] for send in sends], *held)
        rows = rows[: len(sends)] if len(sends) + len(held) > 1 else [rows]
        self.order.leave(*rows)
        for name in names:
            self.got[name] = []
        self.done.append([])
        for row, (name, _, forward) in zip(rows, sends):
            got = step(row, forward)
            self.got[name].append(got)
            self.done[-1].append(got)

    def drain(self):
        arrived = [got for some in self.done[-2:] for got in some]
        self.order.last = (*self.order.last, *arrived)

    def finish(self, name):
        if ringed() and name not in self.results:
            try:
                self.plans[name].send(self.got[name])
            except StopIteration as stop:
                self.results[name] = stop.value
        return self.results[name]

    def load(self, names):
        cuts = []
        row = 0
        for name in names:
            pieces = self.finish(name)
            count, width = pieces[0][1].shape
            cuts += [(row, slot * width, 0, count, block) for slot, block in pieces]
            row += count
        return ((row, width * len(pieces)), cuts)


class Collect:
    def __init__(self, order, rows):
        self.order = order
        self.own = order.wait(rows)
        self.across = swap(self.own, 2)

    def middle(self):
        self.across = self.order.wait(self.across)
        self.corner = swap(self.across, 1)
        self.corner = self.order.wait(self.corner)
        self.core = swap(self.order.wait(self.own), 1)

    def both(self):
        self.across = self.order.wait(self.across)
        self.core = swap(self.own, 1)
        self.corner = swap(self.across, 1)

    def end(self):
        self.core, self.corner = self.order.wait(self.core, self.corner)

    def load(self, seqs=1):
        blocks = (self.own, self.across, self.core, self.corner)
        count = self.own.shape[0] // seqs
        cuts = [
            ((s * len(blocks) + i) * count, 0, s * count, count, block)
            for s in range(seqs)
            for i, block in enumerate(blocks)
        ]
        return ((len(blocks) * self.own.shape[0], self.own.shape[1]), cuts)


def sent_body(near, core, sent):
    count = sent.shape[0]
    sent[...] = (near[count:].astype(f32) + core[count:].astype(f32)).astype(bf16)


class Spread:
    def __init__(self, order, far, near):
        self.order = order
        self.near = near
        self.core = swap(order.wait(far), 1)

    def middle(self):
        count, width = self.near.shape
        sent = self.order.call(
            sent_body, [shaped(count // 2, width)], vmem=(self.near, self.core)
        )
        self.across = swap(sent, 2)

    def end(self):
        self.across = self.order.wait(self.across)

    def terms(self):
        return self.near, self.core, self.across


def total_of(near, core, across):
    count = across.shape[0]
    return near[:count].astype(f32) + core[:count].astype(f32) + across[...].astype(f32)


def turn(values):
    half = values.shape[0] // 2
    return jnp.concatenate([-values[half:], values[:half]], axis=0)


def turn_back(values):
    half = values.shape[0] // 2
    return jnp.concatenate([values[half:], -values[:half]], axis=0)


def head_scale(pre):
    return lax.rsqrt(jnp.mean(pre * pre, axis=0, keepdims=True) + norm_eps)


def row_scale(values):
    return lax.rsqrt(jnp.mean(values * values, axis=-1, keepdims=True) + norm_eps)


def head_prep(pre, gain, cosine, sine):
    scaled = pre * head_scale(pre) * gain
    return scaled * cosine + turn(scaled) * sine


def head_back(grad, pre, gain, cosine, sine):
    grad = grad * cosine + turn_back(grad * sine)
    scale = head_scale(pre)
    lifted = grad * gain
    back = scale * lifted - pre * (scale**3) * jnp.mean(lifted * pre, axis=0, keepdims=True)
    return back, grad * pre * scale


def pick(which, options):
    out = options[0]
    for i in range(1, len(options)):
        out = jnp.where(which == i, options[i], out)
    return out


def put(target, rows, s, seqs, block):
    part = block.shape[1] // len(BLOCKS)
    for i in range(len(BLOCKS)):
        begin = (i * seqs + s) * part
        target[rows, begin : begin + part] = block[:, i * part : (i + 1) * part]


def get(source, rows, s, seqs):
    part = source.shape[1] // (len(BLOCKS) * seqs)
    begins = [(i * seqs + s) * part for i in range(len(BLOCKS))]
    return jnp.concatenate([source[rows, begin : begin + part] for begin in begins], axis=1)


def halves(left, weight, far, near):
    count = near.shape[0]
    near[...] = tn(left[:, :count], weight[...]).astype(bf16)
    far[...] = tn(left[:, count:], weight[...]).astype(bf16)


def x_rows(array, seqs):
    return array.shape[1] // seqs


def from_table(table, span):
    return (
        table[:, 2 * span : 2 * span + 1],
        table[:, 2 * span + 128 : 2 * span + 129],
        table[:, :span],
        table[:, span : 2 * span],
    )


def causal_mask(begins, span):
    part = span // len(BLOCKS)

    def positions(axis):
        at = lax.broadcasted_iota(jnp.int32, (span, span), axis)
        out = at + begins[0]
        for i in range(1, len(BLOCKS)):
            out = jnp.where(at >= i * part, at - i * part + begins[i], out)
        return out

    return positions(1) >= positions(0)


def attend_body(
    heads, kv_local, seqs, kv_of, begins, table, get_x, get_weight,
    far, near, mixed, queries, keys, values, log_total, qkv, scales,
):
    head = table.shape[0]
    span = x_rows(queries, seqs)
    q_gain, k_gain, cosine, sine = from_table(table, span)
    k_base = heads * head
    v_base = k_base + kv_local * head
    rows_all = v_base + kv_local * head
    causal = causal_mask(begins, span)
    x = get_x()
    squares = jnp.zeros((x.shape[0], 128), f32)
    for i in range(x.shape[1] // 128):
        part = x[:, i * 128 : (i + 1) * 128].astype(f32)
        squares = squares + part * part
    sums = nt(jnp.ones((8, 128), f32), squares, lax.Precision.HIGHEST)
    scales[...] = lax.rsqrt(sums[:1] / x.shape[1] + norm_eps)
    weight = get_weight()
    qkv[...] = nt(weight[:rows_all], x[...]) * scales[...]
    for s in range(seqs):
        lanes = slice(s * span, (s + 1) * span)
        key_list = []
        value_list = []
        for c in range(kv_local):
            rows = slice(c * head, (c + 1) * head)
            key = head_prep(
                qkv[k_base + c * head : k_base + (c + 1) * head, lanes],
                k_gain, cosine, sine,
            ).astype(bf16)
            value = qkv[v_base + c * head : v_base + (c + 1) * head, lanes].astype(bf16)
            keys[rows, lanes] = key
            values[rows, lanes] = value
            key_list.append(key)
            value_list.append(value)
        for h in range(heads):
            rows = slice(h * head, (h + 1) * head)
            query = head_prep(qkv[rows, lanes], q_gain, cosine, sine).astype(bf16)
            queries[rows, lanes] = query
            key = pick(kv_of[h], key_list)
            value = pick(kv_of[h], value_list)
            scores = jnp.where(causal, tn(key, query) * head ** (-0.5), masked_score)
            top = jnp.max(scores, axis=0, keepdims=True)
            expos = jnp.exp(scores - top)
            total = jnp.sum(expos, axis=0, keepdims=True)
            log_total[h : h + 1, lanes] = top + jnp.log(total)
            probs = (expos / total).astype(bf16)
            put(mixed, rows, s, seqs, nn(value, probs).astype(bf16))
    halves(mixed, weight[rows_all:], far, near)


def attend_back_body(
    heads, kv_local, seqs, cut, kv_of, begins, qkv, queries, keys, values, log_total, mixed,
    table, scales, get_grad, get_weight, get_x,
    *outs,
):
    grad_blocks, gain_grads, *parts, grad_mixed, grad_qkv = outs
    head = table.shape[0]
    span = x_rows(queries, seqs)
    q_gain, k_gain, cosine, sine = from_table(table, span)
    causal = causal_mask(begins, span)
    k_base = heads * head
    v_base = k_base + kv_local * head
    rows_all = v_base + kv_local * head
    factor = head ** (-0.5)
    q_sum = jnp.zeros((head, span), f32)
    k_sum = jnp.zeros((head, span), f32)
    weight = get_weight()
    grad_rows = get_grad()
    grad_mixed[...] = nt(weight[rows_all:], grad_rows[...]).astype(bf16)
    for s in range(seqs):
        lanes = slice(s * span, (s + 1) * span)
        scale = scales[:, lanes]
        kv_rows = [slice(c * head, (c + 1) * head) for c in range(kv_local)]
        key_list = [keys[rows, lanes] for rows in kv_rows]
        value_list = [values[rows, lanes] for rows in kv_rows]
        grad_keys = [jnp.zeros((head, span), f32) for _ in kv_rows]
        grad_values = [jnp.zeros((head, span), f32) for _ in kv_rows]

        def leave(rows, block, s=s, lanes=lanes, scale=scale):
            block = (block * scale).astype(bf16)
            grad_qkv[rows, lanes] = block
            put(grad_blocks, rows, s, seqs, block)

        for h in range(heads):
            rows = slice(h * head, (h + 1) * head)
            query = queries[rows, lanes]
            grad = get(grad_mixed, rows, s, seqs)
            key = pick(kv_of[h], key_list)
            value = pick(kv_of[h], value_list)
            scores = jnp.where(causal, tn(key, query) * factor, masked_score)
            soft = jnp.exp(scores - log_total[h : h + 1, lanes])
            grad_probs = tn(value, grad)
            inner = jnp.sum(soft * grad_probs, axis=0, keepdims=True)
            grad_scores = (soft * (grad_probs - inner)).astype(bf16)
            grad_query = nn(key, grad_scores) * factor
            grad_key = nt(query, grad_scores) * factor
            grad_value = nt(grad, soft.astype(bf16))
            for c in range(kv_local):
                mine = kv_of[h] == c
                grad_keys[c] = grad_keys[c] + jnp.where(mine, grad_key, 0.0)
                grad_values[c] = grad_values[c] + jnp.where(mine, grad_value, 0.0)
            back, gain = head_back(
                grad_query, qkv[rows, lanes], q_gain, cosine, sine
            )
            q_sum = q_sum + gain
            leave(rows, back)
        for c in range(kv_local):
            rows = slice(k_base + c * head, k_base + (c + 1) * head)
            back, gain = head_back(
                grad_keys[c], qkv[rows, lanes], k_gain, cosine, sine
            )
            k_sum = k_sum + gain
            leave(rows, back)
            leave(slice(v_base + c * head, v_base + (c + 1) * head), grad_values[c])
    gain_grads[:head] = jnp.sum(q_sum, axis=1, keepdims=True)
    gain_grads[head:] = jnp.sum(k_sum, axis=1, keepdims=True)
    x = get_x()
    count = len(parts) // 2
    width = parts[0].shape[1]
    for i in range(count):
        columns = slice(i * width, (i + 1) * width)
        block = nn(grad_qkv[...], x[:, columns]).astype(bf16)
        parts[i][...] = block[:cut]
        parts[count + i][: rows_all - cut] = block[cut:]
        parts[count + i][rows_all - cut :] = nn(mixed[...], grad_rows[:, columns]).astype(bf16)


def input_sum_body(grad_blocks, get_weight, far, near):
    halves(grad_blocks, get_weight().at[: grad_blocks.shape[0]], far, near)


def hidden_grad_body(get_down, get_cot, hidden_grad):
    hidden_grad[...] = nt(get_down()[...], get_cot()[...])


def ffn_body(hidden_grad, get_rows, get_gate, get_up, get_cot, *outs):
    hidden, grad_gate, grad_up, *parts = outs
    rows = get_rows()
    gate = nt(get_gate()[...], rows[...])
    upward = nt(get_up()[...], rows[...])
    sig = jax.nn.sigmoid(gate)
    silu = gate * sig
    hidden[...] = (silu * upward).astype(bf16)
    grad = hidden_grad[...]
    grad_gate[...] = (grad * upward * sig * (1.0 + gate * (1.0 - sig))).astype(bf16)
    grad_up[...] = (grad * silu).astype(bf16)
    cot = get_cot()
    width = parts[0].shape[1]
    for i, part in enumerate(parts):
        part[...] = nn(hidden[...], cot[:, i * width : (i + 1) * width]).astype(bf16)


def ffn_back_body(grad_gate, grad_up, get_gate, get_up, far, near):
    gate_weight = get_gate()
    up_weight = get_up()
    count = near.shape[0]
    for half, target in ((slice(count, None), far), (slice(0, count), near)):
        total = tn(grad_gate[:, half], gate_weight[...]) + tn(grad_up[:, half], up_weight[...])
        target[...] = total.astype(bf16)


def products(left, right, parts):
    width = parts[0].shape[1]
    for i, part in enumerate(parts):
        part[...] = nn(left[...], right[:, i * width : (i + 1) * width]).astype(bf16)


def ffn_parts_body(grad_gate, grad_up, get_rows, *parts):
    rows = get_rows()
    count = len(parts) // 2
    products(grad_gate, rows, parts[:count])
    products(grad_up, rows, parts[count:])


def result_sum_body(hidden, get_down, far, near):
    halves(hidden, get_down(), far, near)


def middle_body(near, core, across, tokens, middle, normed):
    v = tokens[...].astype(f32) + total_of(near, core, across)
    middle[...] = v
    normed[...] = (v * row_scale(v)).astype(bf16)


def grad_middle_body(near, core, across, cot, middle, grad_middle, grad_low):
    lifted = total_of(near, core, across)
    v = middle[...]
    scale = row_scale(v)
    mean = jnp.mean(lifted * v, axis=-1, keepdims=True)
    grad = cot[...].astype(f32) + scale * lifted - v * scale**3 * mean
    grad_middle[...] = grad
    grad_low[...] = grad.astype(bf16)


def input_grad_body(owner, near, core, across, tokens, grad_middle, out):
    lifted = total_of(near, core, across)
    v = tokens[...].astype(f32)
    mean = jnp.mean(lifted * v, axis=-1, keepdims=True)
    store_ring(out, owner, grad_middle[...] + lifted - v * row_scale(v) ** 2 * mean)


def result_body(owner, near, core, across, middle, out):
    store_ring(out, owner, (middle[...] + total_of(near, core, across)).astype(bf16))


def to_ring_body(owner, first, second, first_out, second_out):
    load_ring(first, owner, first_out)
    load_ring(second, owner, second_out)


def sum_of(terms):
    out = terms[0][...].astype(f32)
    for term in terms[1:]:
        out = out + term[...].astype(f32)
    return out


def plain_body(*refs):
    refs[-1][...] = sum_of(refs[:-1])


def ffn_grad_body(gain, weight, *refs):
    *terms, out, norm = refs
    total = sum_of(terms)
    out[...] = total * gain[...]
    norm[...] = jnp.sum(total * weight[...].astype(f32), axis=0, keepdims=True)


def attn_grad_body(q_cols, cut, gain, weight, *refs):
    *terms, q_out, kv_out, out_out, norm = refs
    count = len(terms) // 2
    first = sum_of(terms[:count])
    second = sum_of(terms[count:])
    rows = weight.shape[0]
    out_out[...] = second[rows - cut :]
    second = second[: rows - cut]
    norm[...] = jnp.sum(first * weight[:cut].astype(f32), axis=0, keepdims=True) + jnp.sum(
        second * weight[cut:].astype(f32), axis=0, keepdims=True
    )
    first = first * gain[...]
    second = second * gain[...]
    q_out[...] = first[:q_cols]
    kv_out[: cut - q_cols] = first[q_cols:].astype(bf16)
    kv_out[cut - q_cols :] = second.astype(bf16)


def kv_sum_body(kv_first, kv_local, kv_heads, which, own, core, across, corner, out):
    pieces = [ref[...].astype(f32) for ref in (own, core, across, corner)]
    by_rank = [pick(which[i], pieces) for i in range(len(kv_first))]
    head = own.shape[0] // (2 * kv_local)
    sums = []
    for kind in range(2):
        for c in range(kv_heads):
            total = jnp.zeros((head, own.shape[1]), f32)
            for i, first in enumerate(kv_first):
                spot = c - first
                if 0 <= spot < kv_local:
                    begin = (kind * kv_local + spot) * head
                    total = total + by_rank[i][begin : begin + head]
            sums.append(total)
    out[...] = jnp.concatenate(sums, axis=0).T


def local(
    inputs,
    attn_norm,
    query_weight,
    key_value_weight,
    out_weight,
    ffn_norm,
    gate_weight,
    up_weight,
    down_weight,
    query_gain,
    key_gain,
    cotangent,
):
    ranks = lax.axis_size("tensor")
    rank = lax.axis_index("tensor")
    seqs, span, width = inputs.shape
    head = query_gain.shape[0]
    heads = query_weight.shape[1] // head
    kv_heads = key_value_weight.shape[1] // (2 * head)
    group = heads * ranks // kv_heads
    kv_first = [(i * heads) // group for i in range(ranks)]
    kv_last = [(i * heads + heads - 1) // group for i in range(ranks)]
    kv_local = max(b - a for a, b in zip(kv_first, kv_last)) + 1
    kv_first = [min(a, kv_heads - kv_local) for a in kv_first]
    kv_start = jnp.asarray(np.asarray(kv_first, np.int32))[rank]
    kv_of = (rank * heads + jnp.arange(heads, dtype=jnp.int32)) // group - kv_start
    rows = seqs * span
    units = gate_weight.shape[1]
    slab = gate_weight.shape[0]
    q_cols = heads * head
    kv_cols = kv_local * head
    qkv_rows = q_cols + 2 * kv_cols
    cut = (q_cols + qkv_rows) // 2
    tokens_all = ranks * rows
    owner = owners()
    part_count = slots()
    part_width = width // part_count

    order = Order()
    links = Links(order)
    v = SimpleNamespace()
    attn_gain = attn_norm.astype(f32)[None]
    ffn_gain = ffn_norm.astype(f32)[None]
    half = [shaped(tokens_all // 2, width)] * 2
    part = [shaped(units, part_width)] * part_count
    row_pair = [shaped(rows, width, kind=f32), shaped(rows, width)]
    ffn_out = [shaped(units, slab, kind=f32), shaped(1, slab, kind=f32)]
    bits = [1 << i for i in range(lax.axis_size("dp").bit_length() - 1)]
    links.gather(Ring.down, down_weight, "ahead")

    def prep_attn():
        query, key_value = order(query_weight, key_value_weight)
        key = lax.dynamic_slice_in_dim(key_value, kv_start * head, kv_cols, axis=1)
        value = lax.dynamic_slice_in_dim(key_value, (kv_heads + kv_start) * head, kv_cols, axis=1)
        v.qkv_own = jnp.concatenate([query.T, key.T, value.T], axis=0)
        qkv_shard = (v.qkv_own.astype(f32) * attn_gain).astype(bf16)
        shard_a = qkv_shard[:cut]
        shard_b = jnp.concatenate([qkv_shard[cut:], out_weight])
        order.leave(shard_a, shard_b)
        links.gather(Ring.attn_a, shard_a, "ahead")
        links.gather(Ring.attn_b, shard_b, "behind")

    def prep_rows():
        v.tokens, v.cot = order.call(
            to_ring_body,
            [shaped(rows, width)] * 2,
            smem=(owner,),
            vmem=(inputs.reshape(rows, width), cotangent.reshape(rows, width)),
        )

    def prep_ffn():
        v.gate_own, v.up_own = order(gate_weight.T, up_weight.T)
        gate_shard = (v.gate_own.astype(f32) * ffn_gain).astype(bf16)
        up_shard = (v.up_own.astype(f32) * ffn_gain).astype(bf16)
        order.leave(gate_shard, up_shard)
        links.gather(Ring.gate, gate_shard, "ahead")
        links.gather(Ring.up, up_shard, "behind")

    def prep_table():
        v.begins = (rank ^ jnp.asarray(BLOCKS, jnp.int32)) * span
        positions = v.begins[:, None] + jnp.arange(span, dtype=jnp.int32)[None]
        inverse = rope_base ** (-2.0 * jnp.arange(head // 2, dtype=f32) / head)
        angles = inverse[:, None] * positions.reshape(-1).astype(f32)[None]
        table = jnp.concatenate(
            [
                jnp.concatenate([jnp.cos(angles)] * 2, axis=0),
                jnp.concatenate([jnp.sin(angles)] * 2, axis=0),
                jnp.broadcast_to(query_gain.astype(f32)[:, None], (head, 128)),
                jnp.broadcast_to(key_gain.astype(f32)[:, None], (head, 128)),
            ],
            axis=1,
        )
        v.table = order.wait(table)

    def x_start():
        v.x = Collect(order, v.tokens)

    def cot_start():
        v.cots = Collect(order, v.cot)

    def attend():
        v.far, v.near, v.mixed, v.queries, v.keys, v.values, v.log_total, v.qkv, v.scales = (
            order.call(
                partial(attend_body, heads, kv_local, seqs),
                [
                    *half,
                    shaped(q_cols, tokens_all),
                    shaped(q_cols, tokens_all),
                    shaped(kv_cols, tokens_all),
                    shaped(kv_cols, tokens_all),
                    shaped(heads, tokens_all, kind=f32),
                    shaped(qkv_rows, tokens_all, kind=f32),
                    shaped(1, tokens_all, kind=f32),
                ],
                smem=(kv_of, v.begins),
                vmem=(v.table,),
                loads=(v.x.load(seqs), links.load([Ring.attn_a, Ring.attn_b])),
            )
        )

    def attn_start():
        v.attn = Spread(order, v.far, v.near)

    def middle():
        v.middle, v.normed = order.call(
            middle_body, row_pair, vmem=(*v.attn.terms(), v.tokens)
        )

    def rows_start():
        v.rows = Collect(order, v.normed)

    def hidden_grad():
        v.hidden_grad = order.call(
            hidden_grad_body,
            [shaped(units, tokens_all, kind=f32)],
            loads=(links.load([Ring.down]), v.cots.load()),
        )

    def ffn():
        v.hidden, v.grad_gate, v.grad_up, *parts = order.call(
            ffn_body,
            [*[shaped(units, tokens_all)] * 3, *part],
            vmem=(v.hidden_grad,),
            loads=(v.rows.load(), links.load([Ring.gate]), links.load([Ring.up]), v.cots.load()),
        )
        links.reduce(Ring.down_sum, parts, "ahead")

    def ffn_back():
        v.ffn_far, v.ffn_near = order.call(
            ffn_back_body,
            half,
            vmem=(v.grad_gate, v.grad_up),
            loads=(links.load([Ring.gate]), links.load([Ring.up])),
        )

    def ffn_start():
        v.ffn = Spread(order, v.ffn_far, v.ffn_near)

    def ffn_parts():
        parts = order.call(
            ffn_parts_body, part * 2, vmem=(v.grad_gate, v.grad_up), grant=24 << 20, loads=(v.rows.load(),)
        )
        links.reduce(Ring.gate_sum, parts[:part_count], "behind")
        links.reduce(Ring.up_sum, parts[part_count:], "ahead")

    def grad_middle():
        v.grad_middle, v.grad_low = order.call(
            grad_middle_body, row_pair, vmem=(*v.ffn.terms(), v.cot, v.middle)
        )

    def grad_start():
        v.grad = Collect(order, v.grad_low)

    def result_parts():
        v.result_far, v.result_near = order.call(
            result_sum_body, half, vmem=(v.hidden,), grant=24 << 20, loads=(links.load([Ring.down]),)
        )

    def attend_back():
        attn_part = [shaped(cut, part_width)] * part_count
        attn_part += [shaped(qkv_rows + q_cols - cut, part_width)] * part_count
        v.grad_blocks, gains, *parts, _, _ = order.call(
            partial(attend_back_body, heads, kv_local, seqs, cut),
            [
                shaped(qkv_rows, tokens_all),
                shaped(2 * head, 1, kind=f32),
                *attn_part,
                shaped(q_cols, tokens_all),
                shaped(qkv_rows, tokens_all),
            ],
            smem=(kv_of, v.begins),
            vmem=(v.qkv, v.queries, v.keys, v.values, v.log_total, v.mixed, v.table, v.scales),
            grant=28 << 20,
            loads=(v.grad.load(), links.load([Ring.attn_a, Ring.attn_b]), v.x.load(seqs)),
        )
        v.gains = gains.reshape(1, 2 * head)
        links.reduce(Ring.attn_a_sum, parts[:part_count], "behind")
        links.reduce(Ring.attn_b_sum, parts[part_count:], "ahead")

    def input_parts():
        v.input_far, v.input_near = order.call(
            input_sum_body,
            half,
            vmem=(v.grad_blocks,),
            grant=24 << 20,
            loads=(links.load([Ring.attn_a, Ring.attn_b]),),
        )

    def input_start():
        v.input = Spread(order, v.input_far, v.input_near)

    def input_grad():
        v.input_grad = order.call(
            input_grad_body,
            [shaped(rows, width, kind=f32)],
            smem=(owner,),
            vmem=(*v.input.terms(), v.tokens, v.grad_middle),
            direct=(0,),
        )

    def result_start():
        v.result = Spread(order, v.result_far, v.result_near)

    def result():
        v.output = order.call(
            result_body,
            [shaped(rows, width)],
            smem=(owner,),
            vmem=(*v.result.terms(), v.middle),
            direct=(0,),
        )

    def gains_0():
        v.gains_step = swap(order.wait(v.gains), bits[0], "dp")

    def gains_1():
        v.gains = order.leave(v.gains + order(v.gains_step))
        v.gains_step = swap(v.gains, bits[1], "dp")

    def gains_2():
        for bit in bits[2:]:
            v.gains = order.leave(v.gains + order(v.gains_step))
            v.gains_step = swap(v.gains, bit, "dp")

    def gains_3():
        v.gains = order.leave(v.gains + order(v.gains_step))

    def gate_sum():
        v.gate_out, v.gate_norm = order.call(
            ffn_grad_body,
            ffn_out,
            vmem=(ffn_gain, v.gate_own, *links.finish(Ring.gate_sum)),
            direct=(0,),
        )

    def up_sum():
        v.up_out, v.up_norm = order.call(
            ffn_grad_body,
            ffn_out,
            vmem=(ffn_gain, v.up_own, *links.finish(Ring.up_sum)),
            direct=(0,),
        )

    def attn_sum():
        v.q_out, v.kv_own, v.out_grad, v.attn_norm_grad = order.call(
            partial(attn_grad_body, q_cols, cut),
            [
                shaped(q_cols, slab, kind=f32),
                shaped(2 * kv_cols, slab),
                shaped(q_cols, slab, kind=f32),
                shaped(1, slab, kind=f32),
            ],
            vmem=(
                attn_gain,
                v.qkv_own,
                *links.finish(Ring.attn_a_sum),
                *links.finish(Ring.attn_b_sum),
            ),
            direct=(0, 2),
        )
        v.across = swap(v.kv_own, 2)
        v.core = swap(v.kv_own, 1)

    def kv_corner():
        v.across = order.wait(v.across)
        v.corner = swap(v.across, 1)

    def kv_sum():
        v.kv_grad = order.call(
            partial(kv_sum_body, kv_first, kv_local, kv_heads),
            [shaped(slab, 2 * kv_heads * head, kind=f32)],
            smem=(rank ^ jnp.arange(ranks, dtype=jnp.int32),),
            vmem=(v.kv_own, v.core, v.across, v.corner),
            direct=(0,),
        )

    def small_start():
        small = jnp.concatenate([v.attn_norm_grad, v.gate_norm + v.up_norm, v.gains], axis=1)
        v.small = order.wait(small)
        v.small_step = swap(v.small, 1)

    def small_middle():
        v.small = order.leave(v.small + order(v.small_step))
        v.small_step = swap(v.small, 2)

    def down_sum():
        v.down_grad = order.call(
            plain_body,
            [shaped(units, slab, kind=f32)],
            vmem=links.finish(Ring.down_sum),
            direct=(0,),
        )

    links.go((Ring.down,))
    prep_attn()
    prep_rows()
    links.go((Ring.attn_a,), 1000)
    x_start()
    links.go((Ring.attn_b,))
    prep_ffn()
    links.go((Ring.attn_a,))
    links.go((Ring.attn_b,))
    v.x.both()
    cot_start()
    links.go((Ring.attn_a,), 3)
    prep_table()
    links.go((Ring.attn_b,))
    links.go((Ring.attn_a, Ring.attn_b))
    links.go((Ring.up,))
    links.go((Ring.gate,))
    attend()
    links.drain()
    links.go((Ring.down,))
    v.cots.middle()
    attn_start()
    v.attn.middle()
    links.go((Ring.gate,))
    links.go((Ring.up,))
    middle()
    rows_start()
    links.go((Ring.down,))
    links.go((Ring.gate,))
    links.go((Ring.down,))
    v.rows.both()
    links.go((Ring.up,))
    hidden_grad()
    links.go((Ring.gate, Ring.up))
    ffn()
    links.go((Ring.down_sum,))
    ffn_back()
    links.go((Ring.down_sum,))
    ffn_start()
    v.ffn.middle()
    ffn_parts()
    links.go((Ring.gate_sum, Ring.up_sum))
    links.go((Ring.down_sum,))
    grad_middle()
    grad_start()
    links.go((Ring.gate_sum,))
    result_parts()
    links.go((Ring.up_sum,))
    result_start()
    v.grad.both()
    links.go((Ring.gate_sum,))
    attend_back()
    links.go((Ring.up_sum,))
    input_parts()
    v.result.middle()
    gains_0()
    links.go((Ring.attn_a_sum, Ring.attn_b_sum))
    links.go((Ring.gate_sum,))
    input_start()
    v.input.middle()
    links.go((Ring.up_sum,))
    links.go((Ring.attn_a_sum,))
    result()
    links.go((Ring.attn_b_sum,))
    gains_1()
    gate_sum()
    v.rows.end()
    links.go((Ring.attn_a_sum,))
    links.go((Ring.attn_b_sum,))
    gains_2()
    links.go((Ring.attn_a_sum,))
    input_grad()
    links.go((Ring.attn_b_sum,))
    up_sum()
    links.go((Ring.down_sum,))
    gains_3()
    attn_sum()
    small_start()
    kv_corner()
    small_middle()
    down_sum()
    kv_sum()

    small = v.small + v.small_step
    return (
        v.output.reshape(inputs.shape),
        v.input_grad.reshape(inputs.shape),
        small[0, :slab],
        v.q_out.T,
        v.kv_grad,
        v.out_grad,
        small[0, slab : 2 * slab],
        v.gate_out.T,
        v.up_out.T,
        v.down_grad,
        small[0, 2 * slab : 2 * slab + head],
        small[0, 2 * slab + head :],
    )


def solution(mesh):
    placed = (
        P("dp", "tensor", None),
        P("dp"),
        P("dp", "tensor"),
        P("dp", None),
        P("tensor", "dp"),
        P("dp"),
        P("dp", "tensor"),
        P("dp", "tensor"),
        P("tensor", "dp"),
        P(),
        P(),
        P("dp", "tensor", None),
    )
    return jax.shard_map(
        local,
        mesh=mesh,
        in_specs=placed,
        out_specs=(
            P("dp", "tensor", None),
            P("dp", "tensor", None),
            P("dp"),
            P("dp", "tensor"),
            P("dp", None),
            P("tensor", "dp"),
            P("dp"),
            P("dp", "tensor"),
            P("dp", "tensor"),
            P("tensor", "dp"),
            P(),
            P(),
        ),
        check_vma=False,
    )
```

```python
from functools import partial
from types import SimpleNamespace

import jax
import jax.numpy as jnp
import numpy as np
from jax import lax
from jax.experimental import pallas as pl
from jax.experimental.pallas import tpu as pltpu
from jax.sharding import PartitionSpec as P

norm_eps = 1e-06
rope_base = 10000.0
masked_score = -1e30
f32 = jnp.float32
bf16 = jnp.bfloat16
big_vmem = 60 * 1024 * 1024
small_vmem = 12 * 1024 * 1024

RING = (0, 2, 4, 6, 7, 5, 3, 1)
OFFSETS = (0, -1, 1, -2, 2, -3, 3, 4)
PLACE = {ring: slot for slot, ring in enumerate(OFFSETS)}
BLOCKS = (0, 2, 1, 3)


class Ring:
    down, attn_a, attn_b, gate, up = range(5)
    down_sum, attn_a_sum, attn_b_sum, gate_sum, up_sum = range(5, 10)


def nn(left, right):
    return lax.dot_general(left, right, (((1,), (0,)), ((), ())), preferred_element_type=f32)


def nt(left, right, precision=None):
    return lax.dot_general(
        left, right, (((1,), (1,)), ((), ())), precision=precision, preferred_element_type=f32
    )


def tn(left, right):
    return lax.dot_general(left, right, (((0,), (0,)), ((), ())), preferred_element_type=f32)


def ringed():
    return lax.axis_size("dp") == len(RING)


def slots():
    return len(RING) if ringed() else 1


def owners():
    if not ringed():
        return jnp.zeros((1,), jnp.int32)
    table = np.zeros((len(RING), len(RING)), np.int32)
    for spot, index in enumerate(RING):
        for slot, offset in enumerate(OFFSETS):
            table[index, slot] = RING[(spot + offset) % len(RING)]
    return jnp.asarray(table)[lax.axis_index("dp")]


def shaped(*shape, kind=bf16):
    return jax.ShapeDtypeStruct(shape, kind)


def call(body, outs, smem=(), vmem=(), loads=(), direct=(), grant=None):
    arrays = []
    index = {}
    plans = []
    for shape, cuts in loads:
        plan = []
        for row, column, first, count, array in cuts:
            if id(array) not in index:
                index[id(array)] = len(arrays)
                arrays.append(array)
            plan.append((row, column, first, count, index[id(array)]))
        plans.append((shape, plan))
    copies = sum(len(plan) for _, plan in plans)

    def kernel(*refs):
        refs = list(refs)
        scalars = [refs.pop(0) for _ in smem]
        blocks = [refs.pop(0) for _ in vmem]
        sources = [refs.pop(0) for _ in arrays]
        finals = [refs.pop(0) for _ in outs]
        targets = list(finals)
        for place in direct:
            targets[place] = refs.pop(0)
        getters = []
        number = 0
        for (_, plan), scratch in zip(plans, refs):
            mine = []
            for row, column, first, count, source in plan:
                width = sources[source].shape[1]
                copy = pltpu.make_async_copy(
                    sources[source].at[pl.ds(first, count)],
                    scratch.at[pl.ds(row, count), pl.ds(column, width)],
                    refs[-1].at[number],
                )
                copy.start()
                mine.append(copy)
                number += 1

            def getter(mine=mine, scratch=scratch):
                for copy in mine:
                    copy.wait()
                return scratch

            getters.append(getter)
        body(*scalars, *blocks, *getters, *targets)
        ends = []
        for place in direct:
            copy = pltpu.make_async_copy(targets[place], finals[place], refs[-1].at[number])
            copy.start()
            ends.append(copy)
            number += 1
        for copy in ends:
            copy.wait()

    scratch = [pltpu.VMEM(outs[place].shape, outs[place].dtype) for place in direct]
    scratch += [pltpu.VMEM(shape, bf16) for shape, _ in plans]
    if scratch:
        scratch.append(pltpu.SemaphoreType.DMA((copies + len(direct),)))
    return pl.pallas_call(
        kernel,
        out_shape=tuple(outs),
        in_specs=[pl.BlockSpec(memory_space=pltpu.SMEM) for _ in smem]
        + [pl.BlockSpec(memory_space=pltpu.VMEM) for _ in vmem]
        + [pl.BlockSpec(memory_space=pl.ANY) for _ in arrays],
        out_specs=tuple(
            pl.BlockSpec(memory_space=pltpu.HBM if i in direct else pltpu.VMEM)
            for i in range(len(outs))
        ),
        scratch_shapes=scratch,
        compiler_params=pltpu.CompilerParams(vmem_limit_bytes=grant or (big_vmem if loads else small_vmem)),
        cost_estimate=pl.CostEstimate(flops=0, bytes_accessed=0, transcendentals=0),
    )(*smem, *vmem, *arrays)


class Order:
    def __init__(self):
        self.last = ()

    def __call__(self, *values):
        out = lax.optimization_barrier((*values, *self.last))[: len(values)]
        return out if len(out) > 1 else out[0]

    def wait(self, *values):
        out = self(*values)
        return self.leave(*out) if len(values) > 1 else self.leave(out)

    def leave(self, *values):
        self.last = values
        return values if len(values) > 1 else values[0]

    def call(self, body, outs, smem=(), vmem=(), loads=(), direct=(), grant=None):
        arrays = [*vmem, *(cut[4] for _, cuts in loads for cut in cuts)]
        held = lax.optimization_barrier((*arrays, *self.last))
        vmem = held[: len(vmem)]
        left = list(held[len(vmem) : len(arrays)])
        seen = {}
        new = []
        for shape, cuts in loads:
            made = []
            for row, column, first, count, array in cuts:
                same = seen.setdefault(id(array), left.pop(0))
                made.append((row, column, first, count, same))
            new.append((shape, made))
        return self.leave(*call(body, outs, smem, vmem, new, direct, grant))


def load_ring(source, owner, target):
    count = slots()
    width = source.shape[1] // count
    for slot in range(count):
        begin = pl.multiple_of(owner[slot] * width, width)
        target[:, slot * width : (slot + 1) * width] = source[:, pl.ds(begin, width)]


def store_ring(target, owner, values):
    count = slots()
    width = target.shape[1] // count
    for slot in range(count):
        begin = pl.multiple_of(owner[slot] * width, width)
        target[:, pl.ds(begin, width)] = values[:, slot * width : (slot + 1) * width]


def step(rows, forward):
    size = len(RING)
    move = 1 if forward else -1
    return lax.ppermute(
        rows, "dp", [(RING[i], RING[(i + move) % size]) for i in range(size)]
    )


def swap(rows, bit, axis="tensor"):
    count = lax.axis_size(axis)
    return lax.ppermute(rows, axis, [(i, i ^ bit) for i in range(count)])


def gather_steps(shard, far):
    pieces = [(PLACE[0], shard)]
    ahead = behind = shard
    for hop in (1, 2, 3):
        ahead, behind = yield [(ahead, True), (behind, False)]
        pieces += [(PLACE[-hop], ahead), (PLACE[hop], behind)]
    (last,) = yield [(ahead, True) if far == "ahead" else (behind, False)]
    pieces.append((PLACE[4], last))
    return pieces


def add_body(*refs):
    count = len(refs) // 3
    for i in range(count):
        total = refs[2 * i][...].astype(f32) + refs[2 * i + 1][...].astype(f32)
        refs[2 * count + i][...] = total.astype(bf16)


def reduce_steps(parts, far, order):
    shape = shaped(*parts[0].shape)

    def part(offset):
        return parts[PLACE[offset]]

    (got,) = yield [(part(4), far == "ahead")]
    ahead, behind = part(3), part(-3)
    if far == "ahead":
        ahead = order.call(add_body, [shape], vmem=(got, ahead))
    else:
        behind = order.call(add_body, [shape], vmem=(got, behind))
    for hop in (2, 1, 0):
        got = yield [(ahead, True), (behind, False)]
        if hop:
            ahead, behind = order.call(
                add_body, [shape] * 2, vmem=(got[0], part(hop), got[1], part(-hop))
            )
    return part(0), *got


class Links:
    def __init__(self, order):
        self.order = order
        self.done = []
        self.plans = {}
        self.got = {}
        self.results = {}

    def gather(self, name, shard, far):
        if ringed():
            self.plans[name] = gather_steps(shard, far)
            self.got[name] = None
        else:
            self.results[name] = [(0, lax.all_gather(shard, "dp", axis=1, tiled=True))]

    def reduce(self, name, parts, far):
        if ringed():
            self.plans[name] = reduce_steps(parts, far, self.order)
            self.got[name] = None
        else:
            total = lax.psum_scatter(parts[0], "dp", scatter_dimension=1, tiled=True)
            self.results[name] = [total]

    def go(self, names, depth=2):
        if not ringed():
            return
        sends = [
            (name, *send) for name in names for send in self.plans[name].send(self.got[name])
        ]
        held = self.done[-depth] if len(self.done) >= depth else []
        rows = self.order(*[send[1] for send in sends], *held)
        rows = rows[: len(sends)] if len(sends) + len(held) > 1 else [rows]
        self.order.leave(*rows)
        for name in names:
            self.got[name] = []
        self.done.append([])
        for row, (name, _, forward) in zip(rows, sends):
            got = step(row, forward)
            self.got[name].append(got)
            self.done[-1].append(got)

    def drain(self):
        arrived = [got for some in self.done[-2:] for got in some]
        self.order.last = (*self.order.last, *arrived)

    def finish(self, name):
        if ringed() and name not in self.results:
            try:
                self.plans[name].send(self.got[name])
            except StopIteration as stop:
                self.results[name] = stop.value
        return self.results[name]

    def load(self, names):
        cuts = []
        row = 0
        for name in names:
            pieces = self.finish(name)
            count, width = pieces[0][1].shape
            cuts += [(row, slot * width, 0, count, block) for slot, block in pieces]
            row += count
        return ((row, width * len(pieces)), cuts)


class Collect:
    def __init__(self, order, rows):
        self.order = order
        self.own = order.wait(rows)
        self.across = swap(self.own, 2)

    def middle(self):
        self.across = self.order.wait(self.across)
        self.corner = swap(self.across, 1)
        self.corner = self.order.wait(self.corner)
        self.core = swap(self.order.wait(self.own), 1)

    def both(self):
        self.across = self.order.wait(self.across)
        self.core = swap(self.own, 1)
        self.corner = swap(self.across, 1)

    def end(self):
        self.core, self.corner = self.order.wait(self.core, self.corner)

    def load(self, seqs=1):
        blocks = (self.own, self.across, self.core, self.corner)
        count = self.own.shape[0] // seqs
        cuts = [
            ((s * len(blocks) + i) * count, 0, s * count, count, block)
            for s in range(seqs)
            for i, block in enumerate(blocks)
        ]
        return ((len(blocks) * self.own.shape[0], self.own.shape[1]), cuts)


def sent_body(near, core, sent):
    count = sent.shape[0]
    sent[...] = (near[count:].astype(f32) + core[count:].astype(f32)).astype(bf16)


class Spread:
    def __init__(self, order, far, near):
        self.order = order
        self.near = near
        self.core = swap(order.wait(far), 1)

    def middle(self):
        count, width = self.near.shape
        sent = self.order.call(
            sent_body, [shaped(count // 2, width)], vmem=(self.near, self.core)
        )
        self.across = swap(sent, 2)

    def end(self):
        self.across = self.order.wait(self.across)

    def terms(self):
        return self.near, self.core, self.across


def total_of(near, core, across):
    count = across.shape[0]
    return near[:count].astype(f32) + core[:count].astype(f32) + across[...].astype(f32)


def turn(values):
    half = values.shape[0] // 2
    return jnp.concatenate([-values[half:], values[:half]], axis=0)


def turn_back(values):
    half = values.shape[0] // 2
    return jnp.concatenate([values[half:], -values[:half]], axis=0)


def head_scale(pre):
    return lax.rsqrt(jnp.mean(pre * pre, axis=0, keepdims=True) + norm_eps)


def row_scale(values):
    return lax.rsqrt(jnp.mean(values * values, axis=-1, keepdims=True) + norm_eps)


def head_prep(pre, gain, cosine, sine):
    scaled = pre * head_scale(pre) * gain
    return scaled * cosine + turn(scaled) * sine


def head_back(grad, pre, gain, cosine, sine):
    grad = grad * cosine + turn_back(grad * sine)
    scale = head_scale(pre)
    lifted = grad * gain
    back = scale * lifted - pre * (scale**3) * jnp.mean(lifted * pre, axis=0, keepdims=True)
    return back, grad * pre * scale


def pick(which, options):
    out = options[0]
    for i in range(1, len(options)):
        out = jnp.where(which == i, options[i], out)
    return out


def put(target, rows, s, seqs, block):
    part = block.shape[1] // len(BLOCKS)
    for i in range(len(BLOCKS)):
        begin = (i * seqs + s) * part
        target[rows, begin : begin + part] = block[:, i * part : (i + 1) * part]


def get(source, rows, s, seqs):
    part = source.shape[1] // (len(BLOCKS) * seqs)
    begins = [(i * seqs + s) * part for i in range(len(BLOCKS))]
    return jnp.concatenate([source[rows, begin : begin + part] for begin in begins], axis=1)


def halves(left, weight, far, near):
    count = near.shape[0]
    near[...] = tn(left[:, :count], weight[...]).astype(bf16)
    far[...] = tn(left[:, count:], weight[...]).astype(bf16)


def x_rows(array, seqs):
    return array.shape[1] // seqs


def from_table(table, span):
    return (
        table[:, 2 * span : 2 * span + 1],
        table[:, 2 * span + 128 : 2 * span + 129],
        table[:, :span],
        table[:, span : 2 * span],
    )


def causal_mask(begins, span):
    part = span // len(BLOCKS)

    def positions(axis):
        at = lax.broadcasted_iota(jnp.int32, (span, span), axis)
        out = at + begins[0]
        for i in range(1, len(BLOCKS)):
            out = jnp.where(at >= i * part, at - i * part + begins[i], out)
        return out

    return positions(1) >= positions(0)


def attend_body(
    heads, kv_local, seqs, kv_of, begins, table, get_x, get_weight,
    far, near, mixed, queries, keys, values, log_total, qkv, scales,
):
    head = table.shape[0]
    span = x_rows(queries, seqs)
    q_gain, k_gain, cosine, sine = from_table(table, span)
    k_base = heads * head
    v_base = k_base + kv_local * head
    rows_all = v_base + kv_local * head
    causal = causal_mask(begins, span)
    x = get_x()
    squares = jnp.zeros((x.shape[0], 128), f32)
    for i in range(x.shape[1] // 128):
        part = x[:, i * 128 : (i + 1) * 128].astype(f32)
        squares = squares + part * part
    sums = nt(jnp.ones((8, 128), f32), squares, lax.Precision.HIGHEST)
    scales[...] = lax.rsqrt(sums[:1] / x.shape[1] + norm_eps)
    weight = get_weight()
    qkv[...] = nt(weight[:rows_all], x[...]) * scales[...]
    for s in range(seqs):
        lanes = slice(s * span, (s + 1) * span)
        key_list = []
        value_list = []
        for c in range(kv_local):
            rows = slice(c * head, (c + 1) * head)
            key = head_prep(
                qkv[k_base + c * head : k_base + (c + 1) * head, lanes],
                k_gain, cosine, sine,
            ).astype(bf16)
            value = qkv[v_base + c * head : v_base + (c + 1) * head, lanes].astype(bf16)
            keys[rows, lanes] = key
            values[rows, lanes] = value
            key_list.append(key)
            value_list.append(value)
        for h in range(heads):
            rows = slice(h * head, (h + 1) * head)
            query = head_prep(qkv[rows, lanes], q_gain, cosine, sine).astype(bf16)
            queries[rows, lanes] = query
            key = pick(kv_of[h], key_list)
            value = pick(kv_of[h], value_list)
            scores = jnp.where(causal, tn(key, query) * head ** (-0.5), masked_score)
            top = jnp.max(scores, axis=0, keepdims=True)
            expos = jnp.exp(scores - top)
            total = jnp.sum(expos, axis=0, keepdims=True)
            log_total[h : h + 1, lanes] = top + jnp.log(total)
            probs = (expos / total).astype(bf16)
            put(mixed, rows, s, seqs, nn(value, probs).astype(bf16))
    halves(mixed, weight[rows_all:], far, near)


def attend_back_body(
    heads, kv_local, seqs, cut, kv_of, begins, qkv, queries, keys, values, log_total, mixed,
    table, scales, get_grad, get_weight, get_x,
    *outs,
):
    grad_blocks, gain_grads, *parts, grad_mixed, grad_qkv = outs
    head = table.shape[0]
    span = x_rows(queries, seqs)
    q_gain, k_gain, cosine, sine = from_table(table, span)
    causal = causal_mask(begins, span)
    k_base = heads * head
    v_base = k_base + kv_local * head
    rows_all = v_base + kv_local * head
    factor = head ** (-0.5)
    q_sum = jnp.zeros((head, span), f32)
    k_sum = jnp.zeros((head, span), f32)
    weight = get_weight()
    grad_rows = get_grad()
    grad_mixed[...] = nt(weight[rows_all:], grad_rows[...]).astype(bf16)
    for s in range(seqs):
        lanes = slice(s * span, (s + 1) * span)
        scale = scales[:, lanes]
        kv_rows = [slice(c * head, (c + 1) * head) for c in range(kv_local)]
        key_list = [keys[rows, lanes] for rows in kv_rows]
        value_list = [values[rows, lanes] for rows in kv_rows]
        grad_keys = [jnp.zeros((head, span), f32) for _ in kv_rows]
        grad_values = [jnp.zeros((head, span), f32) for _ in kv_rows]

        def leave(rows, block, s=s, lanes=lanes, scale=scale):
            block = (block * scale).astype(bf16)
            grad_qkv[rows, lanes] = block
            put(grad_blocks, rows, s, seqs, block)

        for h in range(heads):
            rows = slice(h * head, (h + 1) * head)
            query = queries[rows, lanes]
            grad = get(grad_mixed, rows, s, seqs)
            key = pick(kv_of[h], key_list)
            value = pick(kv_of[h], value_list)
            scores = jnp.where(causal, tn(key, query) * factor, masked_score)
            soft = jnp.exp(scores - log_total[h : h + 1, lanes])
            grad_probs = tn(value, grad)
            inner = jnp.sum(soft * grad_probs, axis=0, keepdims=True)
            grad_scores = (soft * (grad_probs - inner)).astype(bf16)
            grad_query = nn(key, grad_scores) * factor
            grad_key = nt(query, grad_scores) * factor
            grad_value = nt(grad, soft.astype(bf16))
            for c in range(kv_local):
                mine = kv_of[h] == c
                grad_keys[c] = grad_keys[c] + jnp.where(mine, grad_key, 0.0)
                grad_values[c] = grad_values[c] + jnp.where(mine, grad_value, 0.0)
            back, gain = head_back(
                grad_query, qkv[rows, lanes], q_gain, cosine, sine
            )
            q_sum = q_sum + gain
            leave(rows, back)
        for c in range(kv_local):
            rows = slice(k_base + c * head, k_base + (c + 1) * head)
            back, gain = head_back(
                grad_keys[c], qkv[rows, lanes], k_gain, cosine, sine
            )
            k_sum = k_sum + gain
            leave(rows, back)
            leave(slice(v_base + c * head, v_base + (c + 1) * head), grad_values[c])
    gain_grads[:head] = jnp.sum(q_sum, axis=1, keepdims=True)
    gain_grads[head:] = jnp.sum(k_sum, axis=1, keepdims=True)
    x = get_x()
    count = len(parts) // 2
    width = parts[0].shape[1]
    for i in range(count):
        columns = slice(i * width, (i + 1) * width)
        block = nn(grad_qkv[...], x[:, columns]).astype(bf16)
        parts[i][...] = block[:cut]
        parts[count + i][: rows_all - cut] = block[cut:]
        parts[count + i][rows_all - cut :] = nn(mixed[...], grad_rows[:, columns]).astype(bf16)


def input_sum_body(grad_blocks, get_weight, far, near):
    halves(grad_blocks, get_weight().at[: grad_blocks.shape[0]], far, near)


def hidden_grad_body(get_down, get_cot, hidden_grad):
    hidden_grad[...] = nt(get_down()[...], get_cot()[...])


def ffn_body(hidden_grad, get_rows, get_gate, get_up, get_cot, *outs):
    hidden, grad_gate, grad_up, *parts = outs
    rows = get_rows()
    gate = nt(get_gate()[...], rows[...])
    upward = nt(get_up()[...], rows[...])
    sig = jax.nn.sigmoid(gate)
    silu = gate * sig
    hidden[...] = (silu * upward).astype(bf16)
    grad = hidden_grad[...]
    grad_gate[...] = (grad * upward * sig * (1.0 + gate * (1.0 - sig))).astype(bf16)
    grad_up[...] = (grad * silu).astype(bf16)
    cot = get_cot()
    width = parts[0].shape[1]
    for i, part in enumerate(parts):
        part[...] = nn(hidden[...], cot[:, i * width : (i + 1) * width]).astype(bf16)


def ffn_back_body(grad_gate, grad_up, get_gate, get_up, far, near):
    gate_weight = get_gate()
    up_weight = get_up()
    count = near.shape[0]
    for half, target in ((slice(count, None), far), (slice(0, count), near)):
        total = tn(grad_gate[:, half], gate_weight[...]) + tn(grad_up[:, half], up_weight[...])
        target[...] = total.astype(bf16)


def products(left, right, parts):
    width = parts[0].shape[1]
    for i, part in enumerate(parts):
        part[...] = nn(left[...], right[:, i * width : (i + 1) * width]).astype(bf16)


def ffn_parts_body(grad_gate, grad_up, get_rows, *parts):
    rows = get_rows()
    count = len(parts) // 2
    products(grad_gate, rows, parts[:count])
    products(grad_up, rows, parts[count:])


def result_sum_body(hidden, get_down, far, near):
    halves(hidden, get_down(), far, near)


def middle_body(near, core, across, tokens, middle, normed):
    v = tokens[...].astype(f32) + total_of(near, core, across)
    middle[...] = v
    normed[...] = (v * row_scale(v)).astype(bf16)


def grad_middle_body(near, core, across, cot, middle, grad_middle, grad_low):
    lifted = total_of(near, core, across)
    v = middle[...]
    scale = row_scale(v)
    mean = jnp.mean(lifted * v, axis=-1, keepdims=True)
    grad = cot[...].astype(f32) + scale * lifted - v * scale**3 * mean
    grad_middle[...] = grad
    grad_low[...] = grad.astype(bf16)


def input_grad_body(owner, near, core, across, tokens, grad_middle, out):
    lifted = total_of(near, core, across)
    v = tokens[...].astype(f32)
    mean = jnp.mean(lifted * v, axis=-1, keepdims=True)
    store_ring(out, owner, grad_middle[...] + lifted - v * row_scale(v) ** 2 * mean)


def result_body(owner, near, core, across, middle, out):
    store_ring(out, owner, (middle[...] + total_of(near, core, across)).astype(bf16))


def to_ring_body(owner, first, second, first_out, second_out):
    load_ring(first, owner, first_out)
    load_ring(second, owner, second_out)


def sum_of(terms):
    out = terms[0][...].astype(f32)
    for term in terms[1:]:
        out = out + term[...].astype(f32)
    return out


def plain_body(*refs):
    refs[-1][...] = sum_of(refs[:-1])


def ffn_grad_body(gain, weight, *refs):
    *terms, out, norm = refs
    total = sum_of(terms)
    out[...] = total * gain[...]
    norm[...] = jnp.sum(total * weight[...].astype(f32), axis=0, keepdims=True)


def attn_grad_body(q_cols, cut, gain, weight, *refs):
    *terms, q_out, kv_out, out_out, norm = refs
    count = len(terms) // 2
    first = sum_of(terms[:count])
    second = sum_of(terms[count:])
    rows = weight.shape[0]
    out_out[...] = second[rows - cut :]
    second = second[: rows - cut]
    norm[...] = jnp.sum(first * weight[:cut].astype(f32), axis=0, keepdims=True) + jnp.sum(
        second * weight[cut:].astype(f32), axis=0, keepdims=True
    )
    first = first * gain[...]
    second = second * gain[...]
    q_out[...] = first[:q_cols]
    kv_out[: cut - q_cols] = first[q_cols:].astype(bf16)
    kv_out[cut - q_cols :] = second.astype(bf16)


def kv_sum_body(kv_first, kv_local, kv_heads, which, own, core, across, corner, out):
    pieces = [ref[...].astype(f32) for ref in (own, core, across, corner)]
    by_rank = [pick(which[i], pieces) for i in range(len(kv_first))]
    head = own.shape[0] // (2 * kv_local)
    sums = []
    for kind in range(2):
        for c in range(kv_heads):
            total = jnp.zeros((head, own.shape[1]), f32)
            for i, first in enumerate(kv_first):
                spot = c - first
                if 0 <= spot < kv_local:
                    begin = (kind * kv_local + spot) * head
                    total = total + by_rank[i][begin : begin + head]
            sums.append(total)
    out[...] = jnp.concatenate(sums, axis=0).T


def local(
    inputs,
    attn_norm,
    query_weight,
    key_value_weight,
    out_weight,
    ffn_norm,
    gate_weight,
    up_weight,
    down_weight,
    query_gain,
    key_gain,
    cotangent,
):
    ranks = lax.axis_size("tensor")
    rank = lax.axis_index("tensor")
    seqs, span, width = inputs.shape
    head = query_gain.shape[0]
    heads = query_weight.shape[1] // head
    kv_heads = key_value_weight.shape[1] // (2 * head)
    group = heads * ranks // kv_heads
    kv_first = [(i * heads) // group for i in range(ranks)]
    kv_last = [(i * heads + heads - 1) // group for i in range(ranks)]
    kv_local = max(b - a for a, b in zip(kv_first, kv_last)) + 1
    kv_first = [min(a, kv_heads - kv_local) for a in kv_first]
    kv_start = jnp.asarray(np.asarray(kv_first, np.int32))[rank]
    kv_of = (rank * heads + jnp.arange(heads, dtype=jnp.int32)) // group - kv_start
    rows = seqs * span
    units = gate_weight.shape[1]
    slab = gate_weight.shape[0]
    q_cols = heads * head
    kv_cols = kv_local * head
    qkv_rows = q_cols + 2 * kv_cols
    cut = (q_cols + qkv_rows) // 2
    tokens_all = ranks * rows
    owner = owners()
    part_count = slots()
    part_width = width // part_count

    order = Order()
    links = Links(order)
    v = SimpleNamespace()
    attn_gain = attn_norm.astype(f32)[None]
    ffn_gain = ffn_norm.astype(f32)[None]
    half = [shaped(tokens_all // 2, width)] * 2
    part = [shaped(units, part_width)] * part_count
    row_pair = [shaped(rows, width, kind=f32), shaped(rows, width)]
    ffn_out = [shaped(units, slab, kind=f32), shaped(1, slab, kind=f32)]
    bits = [1 << i for i in range(lax.axis_size("dp").bit_length() - 1)]
    links.gather(Ring.down, down_weight, "ahead")

    def prep_attn():
        query, key_value = order(query_weight, key_value_weight)
        key = lax.dynamic_slice_in_dim(key_value, kv_start * head, kv_cols, axis=1)
        value = lax.dynamic_slice_in_dim(key_value, (kv_heads + kv_start) * head, kv_cols, axis=1)
        v.qkv_own = jnp.concatenate([query.T, key.T, value.T], axis=0)
        qkv_shard = (v.qkv_own.astype(f32) * attn_gain).astype(bf16)
        shard_a = qkv_shard[:cut]
        shard_b = jnp.concatenate([qkv_shard[cut:], out_weight])
        order.leave(shard_a, shard_b)
        links.gather(Ring.attn_a, shard_a, "ahead")
        links.gather(Ring.attn_b, shard_b, "behind")

    def prep_rows():
        v.tokens, v.cot = order.call(
            to_ring_body,
            [shaped(rows, width)] * 2,
            smem=(owner,),
            vmem=(inputs.reshape(rows, width), cotangent.reshape(rows, width)),
        )

    def prep_ffn():
        v.gate_own, v.up_own = order(gate_weight.T, up_weight.T)
        gate_shard = (v.gate_own.astype(f32) * ffn_gain).astype(bf16)
        up_shard = (v.up_own.astype(f32) * ffn_gain).astype(bf16)
        order.leave(gate_shard, up_shard)
        links.gather(Ring.gate, gate_shard, "ahead")
        links.gather(Ring.up, up_shard, "behind")

    def prep_table():
        v.begins = (rank ^ jnp.asarray(BLOCKS, jnp.int32)) * span
        positions = v.begins[:, None] + jnp.arange(span, dtype=jnp.int32)[None]
        inverse = rope_base ** (-2.0 * jnp.arange(head // 2, dtype=f32) / head)
        angles = inverse[:, None] * positions.reshape(-1).astype(f32)[None]
        table = jnp.concatenate(
            [
                jnp.concatenate([jnp.cos(angles)] * 2, axis=0),
                jnp.concatenate([jnp.sin(angles)] * 2, axis=0),
                jnp.broadcast_to(query_gain.astype(f32)[:, None], (head, 128)),
                jnp.broadcast_to(key_gain.astype(f32)[:, None], (head, 128)),
            ],
            axis=1,
        )
        v.table = order.wait(table)

    def x_start():
        v.x = Collect(order, v.tokens)

    def cot_start():
        v.cots = Collect(order, v.cot)

    def attend():
        v.far, v.near, v.mixed, v.queries, v.keys, v.values, v.log_total, v.qkv, v.scales = (
            order.call(
                partial(attend_body, heads, kv_local, seqs),
                [
                    *half,
                    shaped(q_cols, tokens_all),
                    shaped(q_cols, tokens_all),
                    shaped(kv_cols, tokens_all),
                    shaped(kv_cols, tokens_all),
                    shaped(heads, tokens_all, kind=f32),
                    shaped(qkv_rows, tokens_all, kind=f32),
                    shaped(1, tokens_all, kind=f32),
                ],
                smem=(kv_of, v.begins),
                vmem=(v.table,),
                loads=(v.x.load(seqs), links.load([Ring.attn_a, Ring.attn_b])),
            )
        )

    def attn_start():
        v.attn = Spread(order, v.far, v.near)

    def middle():
        v.middle, v.normed = order.call(
            middle_body, row_pair, vmem=(*v.attn.terms(), v.tokens)
        )

    def rows_start():
        v.rows = Collect(order, v.normed)

    def hidden_grad():
        v.hidden_grad = order.call(
            hidden_grad_body,
            [shaped(units, tokens_all, kind=f32)],
            loads=(links.load([Ring.down]), v.cots.load()),
        )

    def ffn():
        v.hidden, v.grad_gate, v.grad_up, *parts = order.call(
            ffn_body,
            [*[shaped(units, tokens_all)] * 3, *part],
            vmem=(v.hidden_grad,),
            loads=(v.rows.load(), links.load([Ring.gate]), links.load([Ring.up]), v.cots.load()),
        )
        links.reduce(Ring.down_sum, parts, "ahead")

    def ffn_back():
        v.ffn_far, v.ffn_near = order.call(
            ffn_back_body,
            half,
            vmem=(v.grad_gate, v.grad_up),
            loads=(links.load([Ring.gate]), links.load([Ring.up])),
        )

    def ffn_start():
        v.ffn = Spread(order, v.ffn_far, v.ffn_near)

    def ffn_parts():
        parts = order.call(
            ffn_parts_body, part * 2, vmem=(v.grad_gate, v.grad_up), grant=24 << 20, loads=(v.rows.load(),)
        )
        links.reduce(Ring.gate_sum, parts[:part_count], "behind")
        links.reduce(Ring.up_sum, parts[part_count:], "ahead")

    def grad_middle():
        v.grad_middle, v.grad_low = order.call(
            grad_middle_body, row_pair, vmem=(*v.ffn.terms(), v.cot, v.middle)
        )

    def grad_start():
        v.grad = Collect(order, v.grad_low)

    def result_parts():
        v.result_far, v.result_near = order.call(
            result_sum_body, half, vmem=(v.hidden,), grant=24 << 20, loads=(links.load([Ring.down]),)
        )

    def attend_back():
        attn_part = [shaped(cut, part_width)] * part_count
        attn_part += [shaped(qkv_rows + q_cols - cut, part_width)] * part_count
        v.grad_blocks, gains, *parts, _, _ = order.call(
            partial(attend_back_body, heads, kv_local, seqs, cut),
            [
                shaped(qkv_rows, tokens_all),
                shaped(2 * head, 1, kind=f32),
                *attn_part,
                shaped(q_cols, tokens_all),
                shaped(qkv_rows, tokens_all),
            ],
            smem=(kv_of, v.begins),
            vmem=(v.qkv, v.queries, v.keys, v.values, v.log_total, v.mixed, v.table, v.scales),
            grant=28 << 20,
            loads=(v.grad.load(), links.load([Ring.attn_a, Ring.attn_b]), v.x.load(seqs)),
        )
        v.gains = gains.reshape(1, 2 * head)
        links.reduce(Ring.attn_a_sum, parts[:part_count], "behind")
        links.reduce(Ring.attn_b_sum, parts[part_count:], "ahead")

    def input_parts():
        v.input_far, v.input_near = order.call(
            input_sum_body,
            half,
            vmem=(v.grad_blocks,),
            grant=24 << 20,
            loads=(links.load([Ring.attn_a, Ring.attn_b]),),
        )

    def input_start():
        v.input = Spread(order, v.input_far, v.input_near)

    def input_grad():
        v.input_grad = order.call(
            input_grad_body,
            [shaped(rows, width, kind=f32)],
            smem=(owner,),
            vmem=(*v.input.terms(), v.tokens, v.grad_middle),
            direct=(0,),
        )

    def result_start():
        v.result = Spread(order, v.result_far, v.result_near)

    def result():
        v.output = order.call(
            result_body,
            [shaped(rows, width)],
            smem=(owner,),
            vmem=(*v.result.terms(), v.middle),
            direct=(0,),
        )

    def gains_0():
        v.gains_step = swap(order.wait(v.gains), bits[0], "dp")

    def gains_1():
        v.gains = order.leave(v.gains + order(v.gains_step))
        v.gains_step = swap(v.gains, bits[1], "dp")

    def gains_2():
        for bit in bits[2:]:
            v.gains = order.leave(v.gains + order(v.gains_step))
            v.gains_step = swap(v.gains, bit, "dp")

    def gains_3():
        v.gains = order.leave(v.gains + order(v.gains_step))

    def gate_sum():
        v.gate_out, v.gate_norm = order.call(
            ffn_grad_body,
            ffn_out,
            vmem=(ffn_gain, v.gate_own, *links.finish(Ring.gate_sum)),
            direct=(0,),
        )

    def up_sum():
        v.up_out, v.up_norm = order.call(
            ffn_grad_body,
            ffn_out,
            vmem=(ffn_gain, v.up_own, *links.finish(Ring.up_sum)),
            direct=(0,),
        )

    def attn_sum():
        v.q_out, v.kv_own, v.out_grad, v.attn_norm_grad = order.call(
            partial(attn_grad_body, q_cols, cut),
            [
                shaped(q_cols, slab, kind=f32),
                shaped(2 * kv_cols, slab),
                shaped(q_cols, slab, kind=f32),
                shaped(1, slab, kind=f32),
            ],
            vmem=(
                attn_gain,
                v.qkv_own,
                *links.finish(Ring.attn_a_sum),
                *links.finish(Ring.attn_b_sum),
            ),
            direct=(0, 2),
        )
        v.across = swap(v.kv_own, 2)
        v.core = swap(v.kv_own, 1)

    def kv_corner():
        v.across = order.wait(v.across)
        v.corner = swap(v.across, 1)

    def kv_sum():
        v.kv_grad = order.call(
            partial(kv_sum_body, kv_first, kv_local, kv_heads),
            [shaped(slab, 2 * kv_heads * head, kind=f32)],
            smem=(rank ^ jnp.arange(ranks, dtype=jnp.int32),),
            vmem=(v.kv_own, v.core, v.across, v.corner),
            direct=(0,),
        )

    def small_start():
        small = jnp.concatenate([v.attn_norm_grad, v.gate_norm + v.up_norm, v.gains], axis=1)
        v.small = order.wait(small)
        v.small_step = swap(v.small, 1)

    def small_middle():
        v.small = order.leave(v.small + order(v.small_step))
        v.small_step = swap(v.small, 2)

    def down_sum():
        v.down_grad = order.call(
            plain_body,
            [shaped(units, slab, kind=f32)],
            vmem=links.finish(Ring.down_sum),
            direct=(0,),
        )

    links.go((Ring.down,))
    prep_attn()
    prep_rows()
    links.go((Ring.attn_a,), 1000)
    x_start()
    links.go((Ring.attn_b,))
    prep_ffn()
    links.go((Ring.attn_a,))
    links.go((Ring.attn_b,))
    v.x.both()
    cot_start()
    links.go((Ring.attn_a,), 3)
    prep_table()
    links.go((Ring.attn_b,))
    links.go((Ring.attn_a, Ring.attn_b))
    links.go((Ring.up,))
    links.go((Ring.gate,))
    attend()
    links.drain()
    links.go((Ring.down,))
    attn_start()
    v.cots.middle()
    v.attn.middle()
    links.go((Ring.gate,))
    links.go((Ring.up,))
    middle()
    rows_start()
    links.go((Ring.down,))
    links.go((Ring.gate,))
    links.go((Ring.down,), 3)
    v.rows.both()
    links.go((Ring.up,))
    hidden_grad()
    links.go((Ring.gate, Ring.up))
    ffn()
    links.go((Ring.down_sum,))
    ffn_back()
    links.go((Ring.down_sum,))
    ffn_start()
    v.ffn.middle()
    ffn_parts()
    links.go((Ring.gate_sum, Ring.up_sum))
    links.go((Ring.down_sum,))
    grad_middle()
    grad_start()
    links.go((Ring.gate_sum,))
    result_parts()
    links.go((Ring.up_sum,))
    result_start()
    v.grad.both()
    links.go((Ring.gate_sum,))
    attend_back()
    links.go((Ring.up_sum,))
    input_parts()
    v.result.middle()
    gains_0()
    links.go((Ring.attn_a_sum, Ring.attn_b_sum))
    links.go((Ring.gate_sum,))
    input_start()
    v.input.middle()
    links.go((Ring.up_sum,))
    links.go((Ring.attn_a_sum,))
    result()
    links.go((Ring.attn_b_sum,))
    gate_sum()
    v.rows.end()
    links.go((Ring.attn_a_sum,))
    links.go((Ring.attn_b_sum,))
    gains_1()
    v.x.end()
    gains_2()
    links.go((Ring.attn_a_sum,))
    input_grad()
    links.go((Ring.attn_b_sum,))
    up_sum()
    links.go((Ring.down_sum,))
    gains_3()
    attn_sum()
    v.cots.end()
    small_start()
    kv_corner()
    small_middle()
    down_sum()
    kv_sum()

    small = v.small + v.small_step
    return (
        v.output.reshape(inputs.shape),
        v.input_grad.reshape(inputs.shape),
        small[0, :slab],
        v.q_out.T,
        v.kv_grad,
        v.out_grad,
        small[0, slab : 2 * slab],
        v.gate_out.T,
        v.up_out.T,
        v.down_grad,
        small[0, 2 * slab : 2 * slab + head],
        small[0, 2 * slab + head :],
    )


def solution(mesh):
    placed = (
        P("dp", "tensor", None),
        P("dp"),
        P("dp", "tensor"),
        P("dp", None),
        P("tensor", "dp"),
        P("dp"),
        P("dp", "tensor"),
        P("dp", "tensor"),
        P("tensor", "dp"),
        P(),
        P(),
        P("dp", "tensor", None),
    )
    return jax.shard_map(
        local,
        mesh=mesh,
        in_specs=placed,
        out_specs=(
            P("dp", "tensor", None),
            P("dp", "tensor", None),
            P("dp"),
            P("dp", "tensor"),
            P("dp", None),
            P("tensor", "dp"),
            P("dp"),
            P("dp", "tensor"),
            P("dp", "tensor"),
            P("tensor", "dp"),
            P(),
            P(),
        ),
        check_vma=False,
    )
```
